1024 devices in a mesh: lat: 16 (over z_lo, core), lon: 8 (over y), lev: 8 (over x, z_hi).
Axes of the slice: x: 4, y: 8, z: 16 (z_hi: 2, z_lo: 8; z = z_hi * 8 + z_lo), core: 2. Of those that a mesh axis runs over, the one named last changes fastest.
Arguments:
- outer_increment: bfloat16 [32, 1024, 4096], P('lev', 'lat', 'lon'), may hold values from -6 to 6
- courant: bfloat16 [3, 32, 256, 1024], P(None, 'lev', 'lat', 'lon'), may hold values from -0.29882812 to 0.29882812
- obs_column: int32 [262144], P(('lat', 'lon')), may hold values from 0 to 2047
- obs_level: int32 [262144], P(('lat', 'lon')), may hold values from 0 to 31
- obs_value: float32 [262144], P(('lat', 'lon')), may hold values from -6 to 6
Outputs:
- inner_state: float32 [32, 256, 1024], P('lev', 'lat', 'lon')
- adjoint: float32 [32, 256, 1024], P('lev', 'lat', 'lon')
- outer_next: bfloat16 [32, 1024, 4096], P('lev', 'lat', 'lon')
The draws below stay inside these ranges and needn't reach their ends.
Inputs may be any that keep to these rules, and one draw needn't show every extreme that they name: obs_column numbers a column of the 16 x 512 / 4 inner block of its latitude-longitude block, row by row.
All inputs are finite; a program needn't handle non-finite values.
Results may differ from the reference program's by a relative error of at most 0.001.
Values sent between devices are 32-bit elements; how exact they have to be, the bound alone decides.
No kernel may reach another device: no remote copies, remote signals or barrier semaphores. Data moves between devices by JAX's collectives and lax.ppermute only.
A program may use at most 32 MiB of HBM per device.

```python
import jax
import jax.numpy as jnp

CLAT = 64
CLON = 512
OBS_COL = 2048
NLAT = 1024
NLON = 4096
NLEV = 32
NOBS = 262144
N_LON = 8


def with_ends(drawn, rng, low, top_value):
    index_at = [jax.random.randint(jax.random.fold_in(rng, axis), (), 0, length) for axis, length in enumerate(drawn.shape)]
    widest = drawn.shape.index(max(drawn.shape))
    neighbour = index_at[:widest] + [(index_at[widest] + 1) % drawn.shape[widest]] + index_at[widest + 1:]
    return drawn.at[tuple(index_at)].set(low).at[tuple(neighbour)].set(top_value)


def block_levels(rng, extent, shards, smallest, high):
    gain = 1.0
    for dim, blocks in shards:
        draws = jax.random.uniform(jax.random.fold_in(jax.random.fold_in(rng, 6), dim), (blocks,), jnp.float32, smallest / len(shards), high / len(shards))
        gain = gain * jnp.repeat(jnp.exp(draws), extent[dim] // blocks).reshape((-1,) + (1,) * (len(extent) - 1 - dim))
    return gain


def noise(rng, shape, scale, limit, pieces=(), kind=jnp.bfloat16):
    entries = jax.random.normal(rng, shape, jnp.float32) * scale
    if len(pieces) > 0:
        entries = block_levels(rng, shape, pieces, -0.22, 0.18) * entries
    return jnp.clip(entries, min=-limit, max=limit).astype(kind)


def setup_inputs(seed: int = 0) -> dict:
    keys = jax.random.split(jax.random.key(seed), 6)
    outer_increment = noise(keys[0], (NLEV, NLAT, NLON), 1.0, 6.0, ((0, 8), (1, 16), (2, 8)))
    courant = jnp.clip(jax.random.uniform(keys[1], (3, NLEV, NLAT // 4, NLON // 4), jnp.float32, -0.29882812, 0.29882812) * block_levels(keys[1], (3, NLEV, NLAT // 4, NLON // 4), ((1, 8), (2, 16), (3, 8)), -0.4, 0.0), -0.29882812, 0.29882812).astype(jnp.bfloat16)
    obs_column = with_ends(jax.random.randint(keys[2], (NOBS,), 0, CLAT * CLON // 16), jax.random.fold_in(keys[2], 1), 0, (CLAT * CLON // 16) - 1).astype(jnp.int32)
    obs_level = with_ends(jax.random.randint(keys[3], (NOBS,), 0, NLEV), jax.random.fold_in(keys[3], 1), 0, NLEV - 1).astype(jnp.int32)
    obs_value = noise(keys[4], (NOBS,), 1.0, 6.0, ((0, 128),), jnp.float32)
    return {"outer_increment": outer_increment, "courant": courant, "obs_column": obs_column, "obs_level": obs_level, "obs_value": obs_value}


def extend(field):
    wrapped = jnp.pad(field, ((0, 0), (0, 0), (0, 0), (1, 1)), mode="wrap")
    return jnp.pad(wrapped, ((0, 0), (1, 1), (1, 1), (0, 0)))


def window_of(field, axis, shift):
    sizes = [field.shape[1] - 2, field.shape[2] - 2, field.shape[3] - 2]
    begins = [1, 1, 1]
    begins[axis - 1] = begins[axis - 1] + shift
    return field[:, begins[0]:begins[0] + sizes[0], begins[1]:begins[1] + sizes[1], begins[2]:begins[2] + sizes[2]]


def forward(state, rims_courant):
    numbers = window_of(rims_courant, 1, 0)
    result = (1.0 - jnp.sum(jnp.abs(numbers), axis=0, keepdims=True)) * state
    padded = extend(state)
    for direction in range(3):
        lower = jnp.maximum(numbers[direction:direction + 1], 0.0)
        upper = jnp.maximum(-numbers[direction:direction + 1], 0.0)
        result = result + lower * window_of(padded, direction + 1, -1) + upper * window_of(padded, direction + 1, 1)
    return result


def backward(adjoint, rims_courant):
    numbers = window_of(rims_courant, 1, 0)
    result = (1.0 - jnp.sum(jnp.abs(numbers), axis=0, keepdims=True)) * adjoint
    padded = extend(adjoint)
    for direction in range(3):
        lower = jnp.maximum(rims_courant[direction:direction + 1], 0.0)
        upper = jnp.maximum(-rims_courant[direction:direction + 1], 0.0)
        result = result + window_of(lower * padded, direction + 1, 1) + window_of(upper * padded, direction + 1, -1)
    return result


def reference(outer_increment, courant, obs_column, obs_level, obs_value):
    levels, rows, columns = outer_increment.shape
    inner_rows = rows // 4
    inner_cols = columns // 4
    blocked = outer_increment.reshape(levels, inner_rows, 4, inner_cols, 4)
    coarse = jnp.mean(blocked, axis=(2, 4), dtype=jnp.float32).astype(jnp.float32)
    rims_courant = extend(courant.astype(jnp.float32))
    state = coarse[None]
    for turn in range(2):
        state = forward(state, rims_courant)
    block_rows = CLAT // 4
    block_cols = CLON // 4
    blocks = jnp.arange(obs_column.shape[0], dtype=jnp.int32) // OBS_COL
    row_index = (blocks // N_LON) * block_rows + obs_column // block_cols
    col_index = (blocks % N_LON) * block_cols + obs_column % block_cols
    flat = ((obs_level * inner_rows + row_index) * inner_cols + col_index).astype(jnp.int32)
    innovation = state.reshape(-1)[flat] - obs_value
    forcing = jnp.zeros((levels * inner_rows * inner_cols,), jnp.float32).at[flat].add(innovation)
    adjoint = forcing.reshape(1, levels, inner_rows, inner_cols)
    for turn in range(2):
        adjoint = backward(adjoint, rims_courant)
    spread = jnp.broadcast_to(adjoint[0][:, :, None, :, None], (levels, inner_rows, 4, inner_cols, 4)).reshape(levels, rows, columns)
    outer_next = (outer_increment.astype(jnp.float32) - spread).astype(jnp.bfloat16)
    return state[0], adjoint[0], outer_next
```

```python
import functools

import jax
import jax.numpy as jnp
from jax import lax
from jax.experimental import pallas as pl
from jax.experimental.pallas import tpu as pltpu
from jax.sharding import PartitionSpec as P

F32 = jnp.float32
BF16 = jnp.bfloat16
VMEM = pl.BlockSpec(memory_space=pltpu.VMEM)
SMEM = pl.BlockSpec(memory_space=pltpu.SMEM)

LEV = 4
ROW = 16
COL = 128
DEEP = 12
TALL = 24
OWN = 16 * ROW
NEAR = 40
STRIP = 56


def column_table(wide, narrow, wide_axis):
    shape = (wide, narrow) if wide_axis == 0 else (narrow, wide)
    fine = lax.broadcasted_iota(jnp.int32, shape, wide_axis) >> 2
    coarse = lax.broadcasted_iota(jnp.int32, shape, 1 - wide_axis)
    return (fine == coarse).astype(F32).astype(BF16)


def coarse_kernel(outer_ref, courant_ref, block_ref, up_ref, down_ref, sums_ref):
    sums_ref[...] = jnp.dot(
        outer_ref[...].reshape(LEV * ROW * 4, COL * 4),
        column_table(COL * 4, COL, 0),
        preferred_element_type=F32,
    )
    rows = LEV * ROW
    total = sums_ref[pl.ds(0, rows, stride=4), :]
    for part in range(1, 4):
        total = total + sums_ref[pl.ds(part, rows, stride=4), :]
    block_ref[0:rows, :] = total * 0.0625
    block_ref[rows:OWN, :] = courant_ref[...].astype(F32).reshape(OWN - rows, COL)
    for ref, edge, step in ((up_ref, ROW - 1, -1), (down_ref, 0, 1)):
        for i in range(3):
            ref[4 * i : 4 * i + 4, :] = block_ref[pl.ds(edge + step * i, 4, stride=ROW), :]
        for i in range(2):
            ref[12 + 12 * i : 24 + 12 * i, :] = block_ref[
                pl.ds(rows + edge + step * i, 12, stride=ROW), :
            ]
        ref[36:40, :] = jnp.zeros((4, COL), F32)
        ref[40:44, :] = block_ref[pl.ds(edge + step * 3, 4, stride=ROW), :]
        ref[44:56, :] = block_ref[pl.ds(rows + edge + step * 2, 12, stride=ROW), :]


def obs_kernel(lowest_ref, column_ref, level_ref, value_ref, field_ref, up_ref, down_ref):
    count = column_ref.shape[1]
    chunk = 512
    total = jnp.zeros((4 * COL, COL), F32)
    for begin in range(0, count, chunk):
        cut = slice(begin, begin + chunk)
        cell = column_ref[:, cut]
        place = (level_ref[:, cut] - lowest_ref[0] + 2) * ROW + (cell >> 7)
        value = value_ref[:, cut]
        high = value.astype(BF16).astype(F32)
        rest = value - high
        middle = rest.astype(BF16).astype(F32)
        low = rest - middle
        index = lax.broadcasted_iota(jnp.int32, (COL, chunk), 0)
        here = index == place
        across = jnp.where(index == (cell & 127), 1.0, 0.0).astype(BF16)
        down = jnp.concatenate(
            [jnp.where(here, part, 0.0).astype(BF16) for part in (1.0, high, middle, low)], axis=0
        )
        total = total + lax.dot_general(
            down, across, (((1,), (1,)), ((), ())), preferred_element_type=F32
        )
    field_ref[0:128, :] = total[0:128]
    field_ref[128:256, :] = (total[128:256] + total[256:384]) + total[384:512]
    for ref, edge, step in ((up_ref, ROW - 1, -1), (down_ref, 0, 1)):
        for i in range(2):
            ref[16 * i : 16 * i + 16, :] = field_ref[pl.ds(edge + step * i, 16, stride=ROW), :]


def edge_tiles():
    tiles = []
    for level in range(1, 11):
        off = max(0, 4 - level, level - 7)
        for part in range(3 if off <= 2 else 2):
            tiles.append((0, level, part))
    for k in range(3):
        for level in range(2, 10):
            off = max(0, 4 - level, level - 7)
            for part in range(3 if off <= 1 else 2):
                tiles.append((1 + k, level, part))
    for k in range(2):
        for level in range(3, 9):
            off = max(0, 4 - level, level - 7)
            for part in range(3 if off <= 0 else 2):
                tiles.append((4 + k, level, part))
    return tiles


EDGES = edge_tiles()
PACKS = -(-len(EDGES) // 32)


def gather_kernel(
    parity_ref,
    block_ref,
    before_ref,
    after_ref,
    pair_ref,
    far_ref,
    field_ref,
    field_before_ref,
    field_after_ref,
    all_ref,
    right_ref,
    left_ref,
):
    odd = parity_ref[0]
    pair_level = (1 - odd) * 8
    far_level = odd * 8
    rows = LEV * ROW
    for base, ref in ((4, block_ref), (pair_level, pair_ref), (far_level, far_ref)):
        for f in range(4):
            for l in range(LEV):
                begin = (f * LEV + l) * ROW
                all_ref[f, base + l, 0:ROW, :] = ref[begin : begin + ROW, :]
    for side, (own, offset) in enumerate(((before_ref, OWN), (after_ref, OWN + NEAR))):
        for base, ref, start, reach in (
            (4, own, 0, 4),
            (pair_level, pair_ref, offset, 3),
            (far_level, far_ref, offset, 3),
        ):
            for f in range(4):
                for i in range(reach if f == 0 else reach - 1):
                    if f == 0:
                        begin = 4 * i if i < 3 else 40
                    else:
                        begin = (12 + 12 * i if i < 2 else 44) + (f - 1) * 4
                    row = TALL - 1 - i if side == 0 else ROW + i
                    for l in range(LEV):
                        at = start + begin + l
                        all_ref[f, base + l, row : row + 1, :] = ref[at : at + 1, :]
    for f in range(2):
        for l in range(8):
            begin = (f * 8 + l) * ROW
            all_ref[4 + f, 2 + l, 0:ROW, :] = field_ref[begin : begin + ROW, :]
            for i in range(2):
                at = 16 * i + f * 8 + l
                all_ref[4 + f, 2 + l, TALL - 1 - i : TALL - i, :] = field_before_ref[at : at + 1, :]
                all_ref[4 + f, 2 + l, ROW + i : ROW + i + 1, :] = field_after_ref[at : at + 1, :]
    group = lax.broadcasted_iota(jnp.int32, (8, COL), 1) >> 2
    for pack in range(PACKS):
        right = jnp.zeros((8, COL), F32)
        left = jnp.zeros((8, COL), F32)
        for slot, (f, level, part) in enumerate(EDGES[32 * pack : 32 * pack + 32]):
            tile = all_ref[f, level, 8 * part : 8 * part + 8, :]
            here = group == slot
            right = jnp.where(here, pltpu.roll(tile, (4 * slot + 4) % COL, 1), right)
            left = jnp.where(here, pltpu.roll(tile, 4 * slot, 1) if slot else tile, left)
        right_ref[8 * pack : 8 * pack + 8, :] = right
        left_ref[8 * pack : 8 * pack + 8, :] = left


def turn(tile, shift, axis):
    return pltpu.roll(tile, shift % tile.shape[axis], axis)


def step_kernel(
    all_ref,
    west_ref,
    east_ref,
    outer_ref,
    state_ref,
    adjoint_ref,
    next_ref,
    wide_ref,
    first_ref,
    force_ref,
    back_ref,
    flat_ref,
    spread_ref,
):
    near = lax.broadcasted_iota(jnp.int32, (8, COL), 1) < 64
    wide_ref[:, :, :, 0:COL] = all_ref[...]
    for slot, (f, level, part) in enumerate(EDGES):
        pack, lane = divmod(slot, 32)
        east = east_ref[8 * pack : 8 * pack + 8, :]
        west = west_ref[8 * pack : 8 * pack + 8, :]
        wide_ref[f, level, 8 * part : 8 * part + 8, COL : 2 * COL] = jnp.where(
            near,
            turn(east, -4 * lane, 1) if lane else east,
            turn(west, -4 * lane - 4, 1),
        )

    def plus(x):
        return jnp.maximum(x, 0.0)

    def centre(level):
        return 1.0 - (
            jnp.abs(wide_ref[1, level]) + jnp.abs(wide_ref[2, level]) + jnp.abs(wide_ref[3, level])
        )

    def advance(get, level):
        here = get(level)
        c0, c1, c2 = (wide_ref[1 + k, level] for k in range(3))
        result = centre(level) * here
        result = result + plus(c0) * get(level - 1) + plus(-c0) * get(level + 1)
        result = result + plus(c1) * turn(here, 1, 0) + plus(-c1) * turn(here, -1, 0)
        return result + plus(c2) * turn(here, 1, 1) + plus(-c2) * turn(here, -1, 1)

    def retreat(get, level):
        here = get(level)
        c1, c2 = (wide_ref[2 + k, level] for k in range(2))
        result = centre(level) * here
        result = (
            result
            + plus(wide_ref[1, level + 1]) * get(level + 1)
            + plus(-wide_ref[1, level - 1]) * get(level - 1)
        )
        result = result + turn(plus(c1) * here, -1, 0) + turn(plus(-c1) * here, 1, 0)
        return result + turn(plus(c2) * here, -1, 1) + turn(plus(-c2) * here, 1, 1)

    for level in range(1, 11):
        first_ref[level] = advance(lambda l: wide_ref[0, l], level)
    for level in range(2, 10):
        state = advance(lambda l: first_ref[l], level)
        if 4 <= level < 8:
            state_ref[level - 4] = state[0:ROW, 0:COL]
        force_ref[level] = wide_ref[4, level] * state - wide_ref[5, level]
    for level in range(3, 9):
        back_ref[level] = retreat(lambda l: force_ref[l], level)
    for level in range(4, 8):
        result = retreat(lambda l: back_ref[l], level)[0:ROW, 0:COL]
        adjoint_ref[level - 4] = result
        flat_ref[ROW * (level - 4) : ROW * (level - 3), :] = result
    flat = flat_ref[...]
    high = flat.astype(BF16)
    rest = flat - high.astype(F32)
    middle = rest.astype(BF16)
    low = (rest - middle.astype(F32)).astype(BF16)
    table = column_table(COL * 4, COL, 1)
    spread = jnp.dot(high, table, preferred_element_type=F32)
    spread = spread + jnp.dot(middle, table, preferred_element_type=F32)
    spread = spread + jnp.dot(low, table, preferred_element_type=F32)
    for tile in range(4):
        cut = slice(COL * tile, COL * tile + COL)
        for part in range(4):
            spread_ref[pl.ds(part, LEV * ROW, stride=4), :] = spread[:, cut]
        outer = outer_ref[:, :, cut].astype(F32).reshape(LEV * ROW * 4, COL)
        result = (outer - spread_ref[...]).reshape(LEV, ROW * 4, COL)
        next_ref[:, :, cut] = result.astype(BF16)


def call(kernel, outs, ins, scratch=(), scalars=0, flops=1000000, name=None):
    single = len(outs) == 1
    shapes = [jax.ShapeDtypeStruct(shape, kind) for shape, kind in outs]
    return pl.pallas_call(
        kernel,
        out_shape=shapes[0] if single else shapes,
        in_specs=[SMEM] * scalars + [VMEM] * (len(ins) - scalars),
        out_specs=VMEM if single else [VMEM] * len(outs),
        scratch_shapes=list(scratch),
        compiler_params=pltpu.CompilerParams(vmem_limit_bytes=16 * 1024 * 1024),
        cost_estimate=pl.CostEstimate(flops=flops, bytes_accessed=500000, transcendentals=0),
        name=name,
    )(*ins)


def shift(size, by, wrap):
    return [
        (i, (i + by) % size) for i in range(size) if wrap or 0 <= i + by < size
    ]


def shards(outer_increment, courant, obs_column, obs_level, obs_value):
    lev = lax.axis_size("lev")
    lat_up, lat_down = (shift(lax.axis_size("lat"), by, False) for by in (1, -1))
    lon_up, lon_down = (shift(lax.axis_size("lon"), by, True) for by in (1, -1))
    pairs = [(i, i ^ 1) for i in range(lev)]
    far = [(i, i + 2) for i in range(0, lev - 2, 2)] + [(i, i - 2) for i in range(3, lev, 2)]
    position = lax.axis_index("lev").astype(jnp.int32)
    parity = (position & 1).reshape(1)
    lowest = (position * LEV).reshape(1)

    block, up, down = call(
        coarse_kernel,
        [((OWN, COL), F32), ((STRIP, COL), F32), ((STRIP, COL), F32)],
        [outer_increment, courant],
        [pltpu.VMEM((LEV * ROW * 4, COL), F32)],
        name="coarse",
    )
    before = lax.ppermute(up, "lat", lat_up)
    after = lax.ppermute(down, "lat", lat_down)
    pair = lax.ppermute(
        jnp.concatenate([block, before[:NEAR], after[:NEAR]], axis=0), "lev", pairs
    )
    far_block = lax.ppermute(pair, "lev", far)

    count = obs_column.shape[0]
    fields, fields_up, fields_down = call(
        obs_kernel,
        [((256, COL), F32), ((32, COL), F32), ((32, COL), F32)],
        [lowest]
        + [array.reshape(1, count) for array in (obs_column, obs_level, obs_value)],
        scalars=1,
        name="observe",
    )
    fields_before = lax.ppermute(fields_up, "lat", lat_up)
    fields_after = lax.ppermute(fields_down, "lat", lat_down)

    everything, right, left = call(
        gather_kernel,
        [((6, DEEP, TALL, COL), F32), ((8 * PACKS, COL), F32), ((8 * PACKS, COL), F32)],
        [parity, block, before, after, pair, far_block, fields, fields_before, fields_after],
        scalars=1,
        name="assemble",
    )
    west = lax.ppermute(right, "lon", lon_up)
    east = lax.ppermute(left, "lon", lon_down)
    wide = (DEEP, TALL, 2 * COL)
    state, adjoint, outer_next = call(
        step_kernel,
        [
            ((LEV, ROW, COL), F32),
            ((LEV, ROW, COL), F32),
            (outer_increment.shape, BF16),
        ],
        [everything, west, east, outer_increment],
        [
            pltpu.VMEM((6,) + wide, F32),
            pltpu.VMEM(wide, F32),
            pltpu.VMEM(wide, F32),
            pltpu.VMEM(wide, F32),
            pltpu.VMEM((LEV * ROW, COL), F32),
            pltpu.VMEM((LEV * ROW * 4, COL), F32),
        ],
        name="steps",
    )
    return state, adjoint, outer_next


def solution(mesh):
    placed = (
        P("lev", "lat", "lon"),
        P(None, "lev", "lat", "lon"),
        P(("lat", "lon")),
        P(("lat", "lon")),
        P(("lat", "lon")),
    )
    return jax.shard_map(
        shards,
        mesh=mesh,
        in_specs=placed,
        out_specs=(P("lev", "lat", "lon"), P("lev", "lat", "lon"), P("lev", "lat", "lon")),
        check_vma=False,
    )
```

```python
import jax
import jax.numpy as jnp
from jax import lax
from jax.experimental import pallas as pl
from jax.experimental.pallas import tpu as pltpu
from jax.sharding import PartitionSpec as P

F32 = jnp.float32
BF16 = jnp.bfloat16
VMEM = pl.BlockSpec(memory_space=pltpu.VMEM)
SMEM = pl.BlockSpec(memory_space=pltpu.SMEM)

LEV = 4
ROW = 16
COL = 128
DEEP = 12
TALL = 24
ANY = pl.BlockSpec(memory_space=pl.ANY)
HBM = pl.BlockSpec(memory_space=pltpu.HBM)
PLANES = [(1, 0), (2, 0), (3, 0), (0, 0)]
PLANES += [(f, l) for l in (1, 2) for f in range(4)]
PLANES += [(0, 3), (1, 3), (2, 3), (3, 3)]
OWN = len(PLANES) * ROW
FAR = OWN - 3 * ROW


def reach(f, off):
    return max(0, (4 if f == 0 else 3) - off)


STRIP = [(p, i) for i in range(4) for p, (f, l) in enumerate(PLANES) if i < reach(f, 1 + min(l, 3 - l))]
NEAR = -(-len(STRIP) // 8) * 8
STRIP += [(p, i) for i in range(4) for p, (f, l) in enumerate(PLANES) if i < reach(f, 0) and (p, i) not in STRIP]
TALLY = -(-len(STRIP) // 8) * 8


def column_table(wide, narrow, wide_axis):
    shape = (wide, narrow) if wide_axis == 0 else (narrow, wide)
    fine = lax.broadcasted_iota(jnp.int32, shape, wide_axis) >> 2
    coarse = lax.broadcasted_iota(jnp.int32, shape, 1 - wide_axis)
    return (fine == coarse).astype(F32).astype(BF16)


def coarse_kernel(outer_hbm, courant_hbm, block_ref, up_ref, down_ref, outer_ref, courant_ref, sums_ref, sems):
    copies = [
        pltpu.make_async_copy(outer_hbm, outer_ref, sems.at[0]),
        pltpu.make_async_copy(courant_hbm, courant_ref, sems.at[1]),
    ]
    for copy in copies:
        copy.start()
    table = column_table(COL * 4, COL, 0)
    copies[1].wait()
    for p, (f, l) in enumerate(PLANES):
        if f > 0:
            block_ref[ROW * p : ROW * p + ROW, :] = courant_ref[f - 1, l].astype(F32)
    copies[0].wait()
    sums_ref[...] = jnp.dot(
        outer_ref[...].reshape(LEV * ROW * 4, COL * 4), table, preferred_element_type=F32
    )
    for p, (f, l) in enumerate(PLANES):
        if f == 0:
            total = sums_ref[pl.ds(ROW * 4 * l, ROW, stride=4), :]
            for part in range(1, 4):
                total = total + sums_ref[pl.ds(ROW * 4 * l + part, ROW, stride=4), :]
            block_ref[ROW * p : ROW * p + ROW, :] = total * 0.0625
    for ref, edge, step in ((up_ref, ROW - 1, -1), (down_ref, 0, 1)):
        for at, (p, i) in enumerate(STRIP):
            row = ROW * p + edge + step * i
            ref[at : at + 1, :] = block_ref[row : row + 1, :]
        ref[len(STRIP) : TALLY, :] = jnp.zeros((TALLY - len(STRIP), COL), F32)


def obs_kernel(lowest_ref, column_ref, level_ref, value_ref, field_ref, up_ref, down_ref):
    count = column_ref.shape[1]
    chunk = 512
    total = jnp.zeros((4 * COL, COL), F32)
    for begin in range(0, count, chunk):
        cut = slice(begin, begin + chunk)
        cell = column_ref[:, cut]
        place = (level_ref[:, cut] - lowest_ref[0] + 2) * ROW + (cell >> 7)
        value = value_ref[:, cut]
        high = value.astype(BF16).astype(F32)
        rest = value - high
        middle = rest.astype(BF16).astype(F32)
        low = rest - middle
        index = lax.broadcasted_iota(jnp.int32, (COL, chunk), 0)
        here = index == place
        across = jnp.where(index == (cell & 127), 1.0, 0.0).astype(BF16)
        down = jnp.concatenate(
            [jnp.where(here, part, 0.0).astype(BF16) for part in (1.0, high, middle, low)], axis=0
        )
        total = total + lax.dot_general(
            down, across, (((1,), (1,)), ((), ())), preferred_element_type=F32
        )
    field_ref[0:128, :] = total[0:128]
    field_ref[128:256, :] = (total[128:256] + total[256:384]) + total[384:512]
    for ref, edge, step in ((up_ref, ROW - 1, -1), (down_ref, 0, 1)):
        for i in range(2):
            ref[16 * i : 16 * i + 16, :] = field_ref[pl.ds(edge + step * i, 16, stride=ROW), :]


def edge_tiles():
    tiles = []
    for level in range(1, 11):
        off = max(0, 4 - level, level - 7)
        for part in range(3 if off <= 2 else 2):
            tiles.append((0, level, part))
    for k in range(3):
        for level in range(2, 10):
            off = max(0, 4 - level, level - 7)
            for part in range(3 if off <= 1 else 2):
                tiles.append((1 + k, level, part))
    for k in range(2):
        for level in range(3, 9):
            off = max(0, 4 - level, level - 7)
            for part in range(3 if off <= 0 else 2):
                tiles.append((4 + k, level, part))
    return tiles


EDGES = edge_tiles()
PACKS = -(-len(EDGES) // 32)


def join_kernel(before_ref, after_ref, strips_ref, own_ref):
    for side, ref in enumerate((before_ref, after_ref)):
        strips_ref[NEAR * side : NEAR * side + NEAR, :] = ref[0:NEAR, :]
        own_ref[TALLY * side : TALLY * side + TALLY, :] = ref[...]


def forward_kernel(parity_ref, pair_ref, strips_ref, first_ref, second_ref, far_ref):
    begin = pl.multiple_of((1 - parity_ref[0]) * (3 * ROW), ROW)
    far_ref[0:FAR, :] = pair_ref[pl.ds(begin, FAR), :]
    far_ref[FAR:, :] = strips_ref[...]


def gather_kernel(
    parity_ref,
    block_ref,
    own_ref,
    pair_ref,
    strips_ref,
    far_ref,
    field_ref,
    field_before_ref,
    field_after_ref,
    all_ref,
    right_ref,
    left_ref,
):
    odd = parity_ref[0]
    pair_level = (1 - odd) * 8
    far_level = odd * 8
    for p, (f, l) in enumerate(PLANES):
        begin = ROW * p
        all_ref[f, 4 + l, 0:ROW, :] = block_ref[begin : begin + ROW, :]
        all_ref[f, pair_level + l, 0:ROW, :] = pair_ref[begin : begin + ROW, :]
        begin = pl.multiple_of(jnp.clip(begin - (1 - odd) * (3 * ROW), 0, FAR - ROW), ROW)
        all_ref[f, far_level + l, 0:ROW, :] = far_ref[pl.ds(begin, ROW), :]
    for side in range(2):
        for at, (p, i) in enumerate(STRIP):
            f, l = PLANES[p]
            row = TALL - 1 - i if side == 0 else ROW + i
            begin = TALLY * side + at
            all_ref[f, 4 + l, row : row + 1, :] = own_ref[begin : begin + 1, :]
            if at < NEAR and i < reach(f, 1 + min(l, 3 - l)):
                at += NEAR * side
                all_ref[f, pair_level + l, row : row + 1, :] = strips_ref[at : at + 1, :]
                at += FAR
                all_ref[f, far_level + l, row : row + 1, :] = far_ref[at : at + 1, :]
    for f in range(2):
        for l in range(8):
            begin = (f * 8 + l) * ROW
            all_ref[4 + f, 2 + l, 0:ROW, :] = field_ref[begin : begin + ROW, :]
            for i in range(2):
                at = 16 * i + f * 8 + l
                all_ref[4 + f, 2 + l, TALL - 1 - i : TALL - i, :] = field_before_ref[at : at + 1, :]
                all_ref[4 + f, 2 + l, ROW + i : ROW + i + 1, :] = field_after_ref[at : at + 1, :]
    group = lax.broadcasted_iota(jnp.int32, (8, COL), 1) >> 2
    for pack in range(PACKS):
        right = jnp.zeros((8, COL), F32)
        left = jnp.zeros((8, COL), F32)
        for slot, (f, level, part) in enumerate(EDGES[32 * pack : 32 * pack + 32]):
            tile = all_ref[f, level, 8 * part : 8 * part + 8, :]
            here = group == slot
            right = jnp.where(here, pltpu.roll(tile, (4 * slot + 4) % COL, 1), right)
            left = jnp.where(here, pltpu.roll(tile, 4 * slot, 1) if slot else tile, left)
        right_ref[8 * pack : 8 * pack + 8, :] = right
        left_ref[8 * pack : 8 * pack + 8, :] = left


def turn(tile, shift, axis):
    return pltpu.roll(tile, shift % tile.shape[axis], axis)


def step_kernel(
    all_ref,
    west_ref,
    east_ref,
    outer_ref,
    state_ref,
    adjoint_ref,
    next_ref,
    wide_ref,
    first_ref,
    force_ref,
    back_ref,
    flat_ref,
    spread_ref,
):
    near = lax.broadcasted_iota(jnp.int32, (8, COL), 1) < 64
    wide_ref[:, :, :, 0:COL] = all_ref[...]
    for slot, (f, level, part) in enumerate(EDGES):
        pack, lane = divmod(slot, 32)
        east = east_ref[8 * pack : 8 * pack + 8, :]
        west = west_ref[8 * pack : 8 * pack + 8, :]
        wide_ref[f, level, 8 * part : 8 * part + 8, COL : 2 * COL] = jnp.where(
            near,
            turn(east, -4 * lane, 1) if lane else east,
            turn(west, -4 * lane - 4, 1),
        )

    def plus(x):
        return jnp.maximum(x, 0.0)

    def centre(level):
        return 1.0 - (
            jnp.abs(wide_ref[1, level]) + jnp.abs(wide_ref[2, level]) + jnp.abs(wide_ref[3, level])
        )

    def advance(get, level):
        here = get(level)
        c0, c1, c2 = (wide_ref[1 + k, level] for k in range(3))
        result = centre(level) * here
        result = result + plus(c0) * get(level - 1) + plus(-c0) * get(level + 1)
        result = result + plus(c1) * turn(here, 1, 0) + plus(-c1) * turn(here, -1, 0)
        return result + plus(c2) * turn(here, 1, 1) + plus(-c2) * turn(here, -1, 1)

    def retreat(get, level):
        here = get(level)
        c1, c2 = (wide_ref[2 + k, level] for k in range(2))
        result = centre(level) * here
        result = (
            result
            + plus(wide_ref[1, level + 1]) * get(level + 1)
            + plus(-wide_ref[1, level - 1]) * get(level - 1)
        )
        result = result + turn(plus(c1) * here, -1, 0) + turn(plus(-c1) * here, 1, 0)
        return result + turn(plus(c2) * here, -1, 1) + turn(plus(-c2) * here, 1, 1)

    for level in range(1, 11):
        first_ref[level] = advance(lambda l: wide_ref[0, l], level)
    for level in range(2, 10):
        state = advance(lambda l: first_ref[l], level)
        if 4 <= level < 8:
            state_ref[level - 4] = state[0:ROW, 0:COL]
        force_ref[level] = wide_ref[4, level] * state - wide_ref[5, level]
    for level in range(3, 9):
        back_ref[level] = retreat(lambda l: force_ref[l], level)
    for level in range(4, 8):
        result = retreat(lambda l: back_ref[l], level)[0:ROW, 0:COL]
        adjoint_ref[level - 4] = result
        flat_ref[ROW * (level - 4) : ROW * (level - 3), :] = result
    flat = flat_ref[...]
    high = flat.astype(BF16)
    rest = flat - high.astype(F32)
    middle = rest.astype(BF16)
    low = (rest - middle.astype(F32)).astype(BF16)
    table = column_table(COL * 4, COL, 1)
    spread = jnp.dot(high, table, preferred_element_type=F32)
    spread = spread + jnp.dot(middle, table, preferred_element_type=F32)
    spread = spread + jnp.dot(low, table, preferred_element_type=F32)
    for tile in range(4):
        cut = slice(COL * tile, COL * tile + COL)
        for part in range(4):
            spread_ref[pl.ds(part, LEV * ROW, stride=4), :] = spread[:, cut]
        outer = outer_ref[:, :, cut].astype(F32).reshape(LEV * ROW * 4, COL)
        result = (outer - spread_ref[...]).reshape(LEV, ROW * 4, COL)
        next_ref[:, :, cut] = result.astype(BF16)


def call(kernel, outs, ins, scratch=(), scalars=0, places={}, flops=1000000, name=None):
    single = len(outs) == 1
    shapes = [jax.ShapeDtypeStruct(shape, kind) for shape, kind in outs]
    return pl.pallas_call(
        kernel,
        out_shape=shapes[0] if single else shapes,
        in_specs=[SMEM if i < scalars else places.get(i, VMEM) for i in range(len(ins))],
        out_specs=VMEM if single else [VMEM] * len(outs),
        scratch_shapes=list(scratch),
        compiler_params=pltpu.CompilerParams(vmem_limit_bytes=16 * 1024 * 1024),
        cost_estimate=pl.CostEstimate(flops=flops, bytes_accessed=500000, transcendentals=0),
        name=name,
    )(*ins)


def shift(size, by, wrap):
    return [
        (i, (i + by) % size) for i in range(size) if wrap or 0 <= i + by < size
    ]


def shards(outer_increment, courant, obs_column, obs_level, obs_value):
    lev = lax.axis_size("lev")
    lat_up, lat_down = (shift(lax.axis_size("lat"), by, False) for by in (1, -1))
    lon_up, lon_down = (shift(lax.axis_size("lon"), by, True) for by in (1, -1))
    pairs = [(i, i ^ 1) for i in range(lev)]
    far = [(i, i + 2) for i in range(0, lev - 2, 2)] + [(i, i - 2) for i in range(3, lev, 2)]
    position = lax.axis_index("lev").astype(jnp.int32)
    parity = (position & 1).reshape(1)
    lowest = (position * LEV).reshape(1)

    block, up, down = call(
        coarse_kernel,
        [((OWN, COL), F32), ((TALLY, COL), F32), ((TALLY, COL), F32)],
        [outer_increment, courant],
        [
            pltpu.VMEM(outer_increment.shape, BF16),
            pltpu.VMEM(courant.shape, BF16),
            pltpu.VMEM((LEV * ROW * 4, COL), F32),
            pltpu.SemaphoreType.DMA((2,)),
        ],
        places={0: HBM, 1: HBM},
        name="coarse",
    )
    pair = lax.ppermute(block, "lev", pairs)
    before = lax.ppermute(up, "lat", lat_up)
    after = lax.ppermute(down, "lat", lat_down)
    near, own = call(
        join_kernel,
        [((2 * NEAR, COL), F32), ((2 * TALLY, COL), F32)],
        [before, after],
        name="join",
    )
    strips = lax.ppermute(near, "lev", pairs)

    count = obs_column.shape[0]
    fields, fields_up, fields_down = call(
        obs_kernel,
        [((256, COL), F32), ((32, COL), F32), ((32, COL), F32)],
        [lowest]
        + [array.reshape(1, count) for array in (obs_column, obs_level, obs_value)],
        scalars=1,
        name="observe",
    )
    fields_before = lax.ppermute(fields_up, "lat", lat_up)
    fields_after = lax.ppermute(fields_down, "lat", lat_down)

    onward = call(
        forward_kernel,
        [((FAR + 2 * NEAR, COL), F32)],
        [parity, pair, strips, fields_before, fields_after],
        scalars=1,
        places={3: ANY, 4: ANY},
        name="forward",
    )
    far_block = lax.ppermute(onward, "lev", far)
    everything, right, left = call(
        gather_kernel,
        [((6, DEEP, TALL, COL), F32), ((8 * PACKS, COL), F32), ((8 * PACKS, COL), F32)],
        [parity, block, own, pair, strips, far_block, fields, fields_before, fields_after],
        scalars=1,
        name="assemble",
    )
    west = lax.ppermute(right, "lon", lon_up)
    east = lax.ppermute(left, "lon", lon_down)
    wide = (DEEP, TALL, 2 * COL)
    state, adjoint, outer_next = call(
        step_kernel,
        [
            ((LEV, ROW, COL), F32),
            ((LEV, ROW, COL), F32),
            (outer_increment.shape, BF16),
        ],
        [everything, west, east, outer_increment],
        [
            pltpu.VMEM((6,) + wide, F32),
            pltpu.VMEM(wide, F32),
            pltpu.VMEM(wide, F32),
            pltpu.VMEM(wide, F32),
            pltpu.VMEM((LEV * ROW, COL), F32),
            pltpu.VMEM((LEV * ROW * 4, COL), F32),
        ],
        name="steps",
    )
    return state, adjoint, outer_next


def solution(mesh):
    placed = (
        P("lev", "lat", "lon"),
        P(None, "lev", "lat", "lon"),
        P(("lat", "lon")),
        P(("lat", "lon")),
        P(("lat", "lon")),
    )
    return jax.shard_map(
        shards,
        mesh=mesh,
        in_specs=placed,
        out_specs=(P("lev", "lat", "lon"), P("lev", "lat", "lon"), P("lev", "lat", "lon")),
        check_vma=False,
    )
```

```python
import jax
import jax.numpy as jnp
from jax import lax
from jax.experimental import pallas as pl
from jax.experimental.pallas import tpu as pltpu
from jax.sharding import PartitionSpec as P

F32 = jnp.float32
BF16 = jnp.bfloat16
VMEM = pl.BlockSpec(memory_space=pltpu.VMEM)
SMEM = pl.BlockSpec(memory_space=pltpu.SMEM)

LEV = 4
ROW = 16
COL = 128
DEEP = 12
TALL = 24
ANY = pl.BlockSpec(memory_space=pl.ANY)
HBM = pl.BlockSpec(memory_space=pltpu.HBM)
PLANES = [(1, 0), (2, 0), (3, 0), (0, 0)]
PLANES += [(f, l) for l in (1, 2) for f in range(4)]
PLANES += [(0, 3), (1, 3), (2, 3), (3, 3)]
OWN = len(PLANES) * ROW
FAR = OWN - 3 * ROW


def reach(f, off):
    return max(0, (4 if f == 0 else 3) - off)


STRIP = [(p, i) for i in range(4) for p, (f, l) in enumerate(PLANES) if i < reach(f, 1 + min(l, 3 - l))]
NEAR = -(-len(STRIP) // 8) * 8
STRIP += [(p, i) for i in range(4) for p, (f, l) in enumerate(PLANES) if i < reach(f, 0) and (p, i) not in STRIP]
TALLY = -(-len(STRIP) // 8) * 8
EDGE = TALLY + 32


def column_table(wide, narrow, wide_axis):
    shape = (wide, narrow) if wide_axis == 0 else (narrow, wide)
    fine = lax.broadcasted_iota(jnp.int32, shape, wide_axis) >> 2
    coarse = lax.broadcasted_iota(jnp.int32, shape, 1 - wide_axis)
    return (fine == coarse).astype(F32).astype(BF16)


def prepare_kernel(
    lowest_ref,
    outer_hbm,
    courant_hbm,
    column_hbm,
    level_hbm,
    value_hbm,
    block_ref,
    field_ref,
    up_ref,
    down_ref,
    outer_ref,
    courant_ref,
    column_ref,
    level_ref,
    value_ref,
    sums_ref,
    sems,
):
    copies = [
        pltpu.make_async_copy(source, target, sems.at[i])
        for i, (source, target) in enumerate(
            (
                (outer_hbm, outer_ref),
                (courant_hbm, courant_ref),
                (column_hbm, column_ref),
                (level_hbm, level_ref),
                (value_hbm, value_ref),
            )
        )
    ]
    for copy in copies:
        copy.start()
    table = column_table(COL * 4, COL, 0)
    copies[1].wait()
    for p, (f, l) in enumerate(PLANES):
        if f > 0:
            block_ref[ROW * p : ROW * p + ROW, :] = courant_ref[f - 1, l].astype(F32)
    for i in (2, 3, 4):
        copies[i].wait()
    observe(lowest_ref[0], column_ref, level_ref, value_ref, field_ref)
    copies[0].wait()
    sums_ref[...] = jnp.dot(
        outer_ref[...].reshape(LEV * ROW * 4, COL * 4), table, preferred_element_type=F32
    )
    for p, (f, l) in enumerate(PLANES):
        if f == 0:
            total = sums_ref[pl.ds(ROW * 4 * l, ROW, stride=4), :]
            for part in range(1, 4):
                total = total + sums_ref[pl.ds(ROW * 4 * l + part, ROW, stride=4), :]
            block_ref[ROW * p : ROW * p + ROW, :] = total * 0.0625
    for ref, edge, step in ((up_ref, ROW - 1, -1), (down_ref, 0, 1)):
        for at, (p, i) in enumerate(STRIP):
            row = ROW * p + edge + step * i
            ref[at : at + 1, :] = block_ref[row : row + 1, :]
        ref[len(STRIP) : TALLY, :] = jnp.zeros((TALLY - len(STRIP), COL), F32)
        for i in range(2):
            begin = TALLY + 16 * i
            ref[begin : begin + 16, :] = field_ref[pl.ds(edge + step * i, 16, stride=ROW), :]


def observe(lowest, column_ref, level_ref, value_ref, field_ref):
    count = column_ref.shape[1]
    chunk = 512
    total = jnp.zeros((4 * COL, COL), F32)
    for begin in range(0, count, chunk):
        cut = slice(begin, begin + chunk)
        cell = column_ref[:, cut]
        place = (level_ref[:, cut] - lowest + 2) * ROW + (cell >> 7)
        value = value_ref[:, cut]
        high = value.astype(BF16).astype(F32)
        rest = value - high
        middle = rest.astype(BF16).astype(F32)
        low = rest - middle
        index = lax.broadcasted_iota(jnp.int32, (COL, chunk), 0)
        here = index == place
        across = jnp.where(index == (cell & 127), 1.0, 0.0).astype(BF16)
        down = jnp.concatenate(
            [jnp.where(here, part, 0.0).astype(BF16) for part in (1.0, high, middle, low)], axis=0
        )
        total = total + lax.dot_general(
            down, across, (((1,), (1,)), ((), ())), preferred_element_type=F32
        )
    field_ref[0:128, :] = total[0:128]
    field_ref[128:256, :] = (total[128:256] + total[256:384]) + total[384:512]


def tile_table():
    own = [(f, l, part) for f in range(4) for l in range(LEV) for part in range(3)]
    first = [(f, l, part) for f, l, part in own if part < 2 or reach(f, 1 + min(l, 3 - l)) > 1]
    tiles = first + [tile for tile in own if tile not in first]
    for f in (4, 5):
        for l in range(1, 7):
            tiles += [(f, l, part) for part in range(3 if 2 <= l < 6 else 2)]
    return tiles, len(first)


TILES, SENT_ON = tile_table()
PACKS = -(-len(TILES) // 32) * 8
ON = -(-SENT_ON // 32) * 8
MORE = 2 * NEAR + 2 * ON


def edges_kernel(block_ref, field_ref, before_ref, after_ref, own_ref, obs_ref, near_ref, right_ref, left_ref):
    for p, (f, l) in enumerate(PLANES):
        own_ref[f, l, 0:ROW, :] = block_ref[ROW * p : ROW * p + ROW, :]
    for f in range(2):
        for l in range(8):
            begin = (f * 8 + l) * ROW
            obs_ref[f, l, 0:ROW, :] = field_ref[begin : begin + ROW, :]
    for side, ref in enumerate((before_ref, after_ref)):
        near_ref[NEAR * side : NEAR * side + NEAR, :] = ref[0:NEAR, :]
        for at, (p, i) in enumerate(STRIP):
            f, l = PLANES[p]
            row = TALL - 1 - i if side == 0 else ROW + i
            own_ref[f, l, row : row + 1, :] = ref[at : at + 1, :]
        for i in range(2):
            row = TALL - 1 - i if side == 0 else ROW + i
            for plane in range(16):
                at = TALLY + 16 * i + plane
                obs_ref[plane // 8, plane % 8, row : row + 1, :] = ref[at : at + 1, :]
    group = lax.broadcasted_iota(jnp.int32, (8, COL), 1) >> 2
    for pack in range(0, PACKS, 8):
        right = jnp.zeros((8, COL), F32)
        left = jnp.zeros((8, COL), F32)
        for slot, (f, l, part) in enumerate(TILES[4 * pack : 4 * pack + 32]):
            ref, f = (own_ref, f) if f < 4 else (obs_ref, f - 4)
            tile = ref[f, l, 8 * part : 8 * part + 8, :]
            right = jnp.where(group == slot, turn(tile, 4 * slot + 4, 1), right)
            left = jnp.where(group == slot, turn(tile, 4 * slot, 1), left)
        right_ref[pack : pack + 8, :] = right
        left_ref[pack : pack + 8, :] = left


def turn(tile, shift, axis):
    shift = shift % tile.shape[axis]
    return pltpu.roll(tile, shift, axis) if shift else tile


def join_kernel(near_ref, west_ref, east_ref, more_ref):
    more_ref[0 : 2 * NEAR, :] = near_ref[...]
    more_ref[2 * NEAR : 2 * NEAR + ON, :] = west_ref[0:ON, :]
    more_ref[2 * NEAR + ON : MORE, :] = east_ref[0:ON, :]


def forward_kernel(parity_ref, pair_ref, more_ref, far_ref):
    begin = pl.multiple_of((1 - parity_ref[0]) * (3 * ROW), ROW)
    far_ref[0:FAR, :] = pair_ref[pl.ds(begin, FAR), :]
    far_ref[FAR:, :] = more_ref[...]


def place_strips(wide_ref, base, ref, start):
    for side in range(2):
        for at, (p, i) in enumerate(STRIP[:NEAR]):
            f, l = PLANES[p]
            if i < reach(f, 1 + min(l, 3 - l)):
                row = TALL - 1 - i if side == 0 else ROW + i
                at += start + NEAR * side
                wide_ref[f, base + l, row : row + 1, 0:COL] = ref[at : at + 1, :]


def place_edges(wide_ref, base, tiles, west, east):
    half = lax.broadcasted_iota(jnp.int32, (8, COL), 1) < 64
    for slot, (f, l, part) in enumerate(tiles):
        pack, lane = divmod(slot, 32)
        level = base + l if f < 4 else 2 + l
        wide_ref[f, level, 8 * part : 8 * part + 8, COL : 2 * COL] = jnp.where(
            half, turn(east(8 * pack), -4 * lane, 1), turn(west(8 * pack), -4 * lane - 4, 1)
        )


def place_more(wide_ref, base, ref, start):
    place_strips(wide_ref, base, ref, start)
    west = start + 2 * NEAR
    place_edges(
        wide_ref,
        base,
        TILES[:SENT_ON],
        lambda row: ref[west + row : west + row + 8, :],
        lambda row: ref[west + ON + row : west + ON + row + 8, :],
    )


def assemble_kernel(parity_ref, own_ref, obs_ref, west_ref, east_ref, pair_ref, more_ref, wide_ref):
    wide_ref[0:4, 4:8, :, 0:COL] = own_ref[...]
    wide_ref[4:6, 2:10, :, 0:COL] = obs_ref[...]
    place_edges(
        wide_ref,
        4,
        TILES,
        lambda row: west_ref[row : row + 8, :],
        lambda row: east_ref[row : row + 8, :],
    )
    base = (1 - parity_ref[0]) * 8
    for p, (f, l) in enumerate(PLANES):
        wide_ref[f, base + l, 0:ROW, 0:COL] = pair_ref[ROW * p : ROW * p + ROW, :]
    place_more(wide_ref, base, more_ref, 0)


def step_kernel(
    parity_ref,
    given_ref,
    far_ref,
    outer_ref,
    state_ref,
    adjoint_ref,
    next_ref,
    wide_ref,
    first_ref,
    force_ref,
    back_ref,
    flat_ref,
    spread_ref,
):
    wide_ref[...] = given_ref[...]
    odd = parity_ref[0]
    for p, (f, l) in enumerate(PLANES):
        begin = pl.multiple_of(jnp.clip(ROW * p - (1 - odd) * (3 * ROW), 0, FAR - ROW), ROW)
        wide_ref[f, odd * 8 + l, 0:ROW, 0:COL] = far_ref[pl.ds(begin, ROW), :]
    place_more(wide_ref, odd * 8, far_ref, FAR)

    def plus(x):
        return jnp.maximum(x, 0.0)

    def centre(level):
        return 1.0 - (
            jnp.abs(wide_ref[1, level]) + jnp.abs(wide_ref[2, level]) + jnp.abs(wide_ref[3, level])
        )

    def advance(get, level):
        here = get(level)
        c0, c1, c2 = (wide_ref[1 + k, level] for k in range(3))
        result = centre(level) * here
        result = result + plus(c0) * get(level - 1) + plus(-c0) * get(level + 1)
        result = result + plus(c1) * turn(here, 1, 0) + plus(-c1) * turn(here, -1, 0)
        return result + plus(c2) * turn(here, 1, 1) + plus(-c2) * turn(here, -1, 1)

    def retreat(get, level):
        here = get(level)
        c1, c2 = (wide_ref[2 + k, level] for k in range(2))
        result = centre(level) * here
        result = (
            result
            + plus(wide_ref[1, level + 1]) * get(level + 1)
            + plus(-wide_ref[1, level - 1]) * get(level - 1)
        )
        result = result + turn(plus(c1) * here, -1, 0) + turn(plus(-c1) * here, 1, 0)
        return result + turn(plus(c2) * here, -1, 1) + turn(plus(-c2) * here, 1, 1)

    for level in range(1, 11):
        first_ref[level] = advance(lambda l: wide_ref[0, l], level)
    for level in range(2, 10):
        state = advance(lambda l: first_ref[l], level)
        if 4 <= level < 8:
            state_ref[level - 4] = state[0:ROW, 0:COL]
        force_ref[level] = wide_ref[4, level] * state - wide_ref[5, level]
    for level in range(3, 9):
        back_ref[level] = retreat(lambda l: force_ref[l], level)
    for level in range(4, 8):
        result = retreat(lambda l: back_ref[l], level)[0:ROW, 0:COL]
        adjoint_ref[level - 4] = result
        flat_ref[ROW * (level - 4) : ROW * (level - 3), :] = result
    flat = flat_ref[...]
    high = flat.astype(BF16)
    rest = flat - high.astype(F32)
    middle = rest.astype(BF16)
    low = (rest - middle.astype(F32)).astype(BF16)
    table = column_table(COL * 4, COL, 1)
    spread = jnp.dot(high, table, preferred_element_type=F32)
    spread = spread + jnp.dot(middle, table, preferred_element_type=F32)
    spread = spread + jnp.dot(low, table, preferred_element_type=F32)
    for tile in range(4):
        cut = slice(COL * tile, COL * tile + COL)
        for part in range(4):
            spread_ref[pl.ds(part, LEV * ROW, stride=4), :] = spread[:, cut]
        outer = outer_ref[:, :, cut].astype(F32).reshape(LEV * ROW * 4, COL)
        result = (outer - spread_ref[...]).reshape(LEV, ROW * 4, COL)
        next_ref[:, :, cut] = result.astype(BF16)


def call(kernel, outs, ins, scratch=(), scalars=0, places={}, cost=500000, name=None):
    single = len(outs) == 1
    shapes = [jax.ShapeDtypeStruct(shape, kind) for shape, kind in outs]
    return pl.pallas_call(
        kernel,
        out_shape=shapes[0] if single else shapes,
        in_specs=[SMEM if i < scalars else places.get(i, VMEM) for i in range(len(ins))],
        out_specs=VMEM if single else [VMEM] * len(outs),
        scratch_shapes=list(scratch),
        compiler_params=pltpu.CompilerParams(vmem_limit_bytes=16 * 1024 * 1024),
        cost_estimate=pl.CostEstimate(flops=cost, bytes_accessed=cost, transcendentals=0),
        name=name,
    )(*ins)


def shift(size, by, wrap):
    return [
        (i, (i + by) % size) for i in range(size) if wrap or 0 <= i + by < size
    ]


def shards(outer_increment, courant, obs_column, obs_level, obs_value):
    lev = lax.axis_size("lev")
    lat_up, lat_down = (shift(lax.axis_size("lat"), by, False) for by in (1, -1))
    lon_up, lon_down = (shift(lax.axis_size("lon"), by, True) for by in (1, -1))
    pairs = [(i, i ^ 1) for i in range(lev)]
    far = [(i, i + 2) for i in range(0, lev - 2, 2)] + [(i, i - 2) for i in range(3, lev, 2)]
    position = lax.axis_index("lev").astype(jnp.int32)
    parity = (position & 1).reshape(1)
    lowest = (position * LEV).reshape(1)

    count = obs_column.shape[0]
    given = [outer_increment, courant]
    given += [array.reshape(1, count) for array in (obs_column, obs_level, obs_value)]
    block, fields, up, down = call(
        prepare_kernel,
        [((OWN, COL), F32), ((OWN, COL), F32), ((EDGE, COL), F32), ((EDGE, COL), F32)],
        [lowest] + [pltpu.with_memory_space_constraint(array, pltpu.HBM) for array in given],
        [pltpu.VMEM(array.shape, array.dtype) for array in given]
        + [pltpu.VMEM((LEV * ROW * 4, COL), F32), pltpu.SemaphoreType.DMA((5,))],
        scalars=1,
        places={i: HBM for i in range(1, 6)},
        name="prepare",
    )
    before = lax.ppermute(up, "lat", lat_up)
    after = lax.ppermute(down, "lat", lat_down)
    pair = lax.ppermute(block, "lev", pairs)
    own, obs, near, right, left = call(
        edges_kernel,
        [
            ((4, LEV, TALL, COL), F32),
            ((2, 8, TALL, COL), F32),
            ((2 * NEAR, COL), F32),
            ((PACKS, COL), F32),
            ((PACKS, COL), F32),
        ],
        [block, fields, before, after],
        cost=500000000,
        name="edges",
    )
    west = lax.ppermute(right, "lon", lon_up)
    east = lax.ppermute(left, "lon", lon_down)
    more = lax.ppermute(
        call(join_kernel, [((MORE, COL), F32)], [near, west, east], cost=500000000, name="join"), "lev", pairs
    )
    onward = call(
        forward_kernel, [((FAR + MORE, COL), F32)], [parity, pair, more], scalars=1, name="forward"
    )
    far_block = lax.ppermute(onward, "lev", far)
    tall = (DEEP, TALL, 2 * COL)
    wide = call(
        assemble_kernel,
        [((6,) + tall, F32)],
        [parity, own, obs, west, east, pair, more],
        scalars=1,
        cost=1000000,
        name="assemble",
    )
    state, adjoint, outer_next = call(
        step_kernel,
        [
            ((LEV, ROW, COL), F32),
            ((LEV, ROW, COL), F32),
            (outer_increment.shape, BF16),
        ],
        [parity, wide, far_block, outer_increment],
        [
            pltpu.VMEM((6,) + tall, F32),
            pltpu.VMEM(tall, F32),
            pltpu.VMEM(tall, F32),
            pltpu.VMEM(tall, F32),
            pltpu.VMEM((LEV * ROW, COL), F32),
            pltpu.VMEM((LEV * ROW * 4, COL), F32),
        ],
        scalars=1,
        name="steps",
    )
    return state, adjoint, outer_next


def solution(mesh):
    placed = (
        P("lev", "lat", "lon"),
        P(None, "lev", "lat", "lon"),
        P(("lat", "lon")),
        P(("lat", "lon")),
        P(("lat", "lon")),
    )
    return jax.shard_map(
        shards,
        mesh=mesh,
        in_specs=placed,
        out_specs=(P("lev", "lat", "lon"), P("lev", "lat", "lon"), P("lev", "lat", "lon")),
        check_vma=False,
    )
```

```python
import jax
import jax.numpy as jnp
from jax import lax
from jax.experimental import pallas as pl
from jax.experimental.pallas import tpu as pltpu
from jax.sharding import PartitionSpec as P

F32 = jnp.float32
BF16 = jnp.bfloat16
VMEM = pl.BlockSpec(memory_space=pltpu.VMEM)
SMEM = pl.BlockSpec(memory_space=pltpu.SMEM)

LEV = 4
ROW = 16
COL = 128
DEEP = 12
TALL = 24
ANY = pl.BlockSpec(memory_space=pl.ANY)
HBM = pl.BlockSpec(memory_space=pltpu.HBM)
PLANES = [(1, 0), (2, 0), (3, 0), (0, 0)]
PLANES += [(f, l) for l in (1, 2) for f in range(4)]
PLANES += [(0, 3), (1, 3), (2, 3), (3, 3)]
OWN = len(PLANES) * ROW
FAR = OWN - 3 * ROW


def reach(f, off):
    return max(0, (4 if f == 0 else 3) - off)


STRIP = [(p, i) for i in range(4) for p, (f, l) in enumerate(PLANES) if i < reach(f, 1 + min(l, 3 - l))]
NEAR = -(-len(STRIP) // 8) * 8
STRIP += [(p, i) for i in range(4) for p, (f, l) in enumerate(PLANES) if i < reach(f, 0) and (p, i) not in STRIP]
TALLY = -(-len(STRIP) // 8) * 8
EDGE = TALLY + 32
CORNERS = EDGE // 8
CORNER_AT = 2 * NEAR
SIDE_AT = CORNER_AT + 16
MORE = SIDE_AT + 16


def column_table(wide, narrow, wide_axis):
    shape = (wide, narrow) if wide_axis == 0 else (narrow, wide)
    fine = lax.broadcasted_iota(jnp.int32, shape, wide_axis) >> 2
    coarse = lax.broadcasted_iota(jnp.int32, shape, 1 - wide_axis)
    return (fine == coarse).astype(F32).astype(BF16)


def prepare_kernel(
    lowest_ref,
    outer_hbm,
    courant_hbm,
    column_hbm,
    level_hbm,
    value_hbm,
    block_ref,
    field_ref,
    right_ref,
    left_ref,
    outer_ref,
    courant_ref,
    column_ref,
    level_ref,
    value_ref,
    sums_ref,
    sems,
):
    copies = [
        pltpu.make_async_copy(source, target, sems.at[i])
        for i, (source, target) in enumerate(
            (
                (outer_hbm, outer_ref),
                (courant_hbm, courant_ref),
                (column_hbm, column_ref),
                (level_hbm, level_ref),
                (value_hbm, value_ref),
            )
        )
    ]
    for copy in copies:
        copy.start()
    table = column_table(COL * 4, COL, 0)
    copies[1].wait()
    for p, (f, l) in enumerate(PLANES):
        if f > 0:
            block_ref[ROW * p : ROW * p + ROW, :] = courant_ref[f - 1, l].astype(F32)
    for i in (2, 3, 4):
        copies[i].wait()
    observe(lowest_ref[0], column_ref, level_ref, value_ref, field_ref)
    copies[0].wait()
    sums_ref[...] = jnp.dot(
        outer_ref[...].reshape(LEV * ROW * 4, COL * 4), table, preferred_element_type=F32
    )
    for p, (f, l) in enumerate(PLANES):
        if f == 0:
            total = sums_ref[pl.ds(ROW * 4 * l, ROW, stride=4), :]
            for part in range(1, 4):
                total = total + sums_ref[pl.ds(ROW * 4 * l + part, ROW, stride=4), :]
            block_ref[ROW * p : ROW * p + ROW, :] = total * 0.0625
    group = lax.broadcasted_iota(jnp.int32, (8, COL), 1) >> 2
    for pack, (ref, begins) in enumerate(((block_ref, BLOCK_TILES), (field_ref, FIELD_TILES))):
        right = jnp.zeros((8, COL), F32)
        left = jnp.zeros((8, COL), F32)
        for slot, begin in enumerate(begins):
            tile = ref[begin : begin + 8, :]
            right = jnp.where(group == slot, turn(tile, 4 * slot + 4, 1), right)
            left = jnp.where(group == slot, turn(tile, 4 * slot, 1), left)
        right_ref[8 * pack : 8 * pack + 8, :] = right
        left_ref[8 * pack : 8 * pack + 8, :] = left


def observe(lowest, column_ref, level_ref, value_ref, field_ref):
    count = column_ref.shape[1]
    chunk = 512
    total = jnp.zeros((4 * COL, COL), F32)
    for begin in range(0, count, chunk):
        cut = slice(begin, begin + chunk)
        cell = column_ref[:, cut]
        place = (level_ref[:, cut] - lowest + 2) * ROW + (cell >> 7)
        value = value_ref[:, cut]
        high = value.astype(BF16).astype(F32)
        rest = value - high
        middle = rest.astype(BF16).astype(F32)
        low = rest - middle
        index = lax.broadcasted_iota(jnp.int32, (COL, chunk), 0)
        here = index == place
        across = jnp.where(index == (cell & 127), 1.0, 0.0).astype(BF16)
        down = jnp.concatenate(
            [jnp.where(here, part, 0.0).astype(BF16) for part in (1.0, high, middle, low)], axis=0
        )
        total = total + lax.dot_general(
            down, across, (((1,), (1,)), ((), ())), preferred_element_type=F32
        )
    field_ref[0:128, :] = total[0:128]
    field_ref[128:256, :] = (total[128:256] + total[256:384]) + total[384:512]


BLOCK_TILES = [8 * t for t in range(OWN // 8)]
FIELD_TILES = [(8 * f + l) * ROW + 8 * part for f in range(2) for l in range(1, 7) for part in range(2)]


def turn(tile, shift, axis):
    shift = shift % tile.shape[axis]
    return pltpu.roll(tile, shift, axis) if shift else tile


def beyond(east, west, slot):
    half = lax.broadcasted_iota(jnp.int32, (8, COL), 1) < 64
    return jnp.where(half, turn(east, -4 * slot, 1), turn(west, -4 * slot - 4, 1))


def strips_kernel(block_ref, field_ref, west_ref, east_ref, up_ref, down_ref, side_ref, strip_ref):
    for pack, begins in enumerate((BLOCK_TILES, FIELD_TILES)):
        rows = slice(8 * pack, 8 * pack + 8)
        east, west = east_ref[rows, :], west_ref[rows, :]
        for slot, begin in enumerate(begins):
            begin += OWN * pack
            side_ref[begin : begin + 8, :] = beyond(east, west, slot)
    group = lax.broadcasted_iota(jnp.int32, (8, COL), 1) >> 3
    for ref, edge, step in ((up_ref, ROW - 1, -1), (down_ref, 0, 1)):
        for at, (p, i) in enumerate(STRIP):
            row = ROW * p + edge + step * i
            ref[at : at + 1, :] = block_ref[row : row + 1, :]
            strip_ref[at : at + 1, :] = side_ref[row : row + 1, :]
        ref[len(STRIP) : TALLY, :] = jnp.zeros((TALLY - len(STRIP), COL), F32)
        for i in range(2):
            begin = TALLY + 16 * i
            row = edge + step * i
            ref[begin : begin + 16, :] = field_ref[pl.ds(row, 16, stride=ROW), :]
            strip_ref[begin : begin + 16, :] = side_ref[pl.ds(OWN + row, 16, stride=ROW), :]
        corners = jnp.zeros((8, COL), F32)
        for j in range(CORNERS):
            tile = strip_ref[8 * j : 8 * j + 8, :]
            corners = jnp.where(group == j, turn(tile, 8 * j + 4, 1), corners)
        ref[EDGE:, :] = corners


def join_kernel(before_ref, after_ref, west_ref, east_ref, more_ref):
    for side, (strip, edge) in enumerate(((before_ref, west_ref), (after_ref, east_ref))):
        more_ref[NEAR * side : NEAR * side + NEAR, :] = strip[0:NEAR, :]
        begin = CORNER_AT + 8 * side
        more_ref[begin : begin + 8, :] = strip[EDGE:, :]
        begin = SIDE_AT + 8 * side
        more_ref[begin : begin + 8, :] = edge[0:8, :]


def forward_kernel(parity_ref, pair_ref, more_ref, far_ref):
    begin = pl.multiple_of((1 - parity_ref[0]) * (3 * ROW), ROW)
    far_ref[0:FAR, :] = pair_ref[pl.ds(begin, FAR), :]
    far_ref[FAR:, :] = more_ref[...]


def place_strip(wide_ref, base, side, strips, wanted, get, corners, corner_ref):
    for j in range(-(-len(strips) // 8)):
        corner_ref[8 * j : 8 * j + 8, :] = turn(corners, -8 * j - 4, 1)
    for at, (p, i) in enumerate(strips):
        f, l = PLANES[p]
        if i < wanted(f, l):
            row = TALL - 1 - i if side == 0 else ROW + i
            wide_ref[f, base + l, row : row + 1, 0:COL] = get(at)
            wide_ref[f, base + l, row : row + 1, COL : 2 * COL] = corner_ref[at : at + 1, :]


def place_more(wide_ref, base, more_ref, corner_ref):
    for side in range(2):
        begin = CORNER_AT + 8 * side
        place_strip(
            wide_ref,
            base,
            side,
            STRIP[:NEAR],
            lambda f, l: reach(f, 1 + min(l, 3 - l)),
            lambda at: more_ref[NEAR * side + at : NEAR * side + at + 1, :],
            more_ref[begin : begin + 8, :],
            corner_ref,
        )
    place_sides(
        wide_ref, base, more_ref[SIDE_AT + 8 : SIDE_AT + 16, :], more_ref[SIDE_AT : SIDE_AT + 8, :]
    )


def place_sides(wide_ref, base, east, west):
    for slot in range(len(BLOCK_TILES)):
        f, l = PLANES[slot // 2]
        rows = slice(8 * (slot % 2), 8 * (slot % 2) + 8)
        wide_ref[f, base + l, rows, COL : 2 * COL] = beyond(east, west, slot)


def assemble_kernel(
    parity_ref,
    block_ref,
    field_ref,
    before_ref,
    after_ref,
    west_ref,
    east_ref,
    pair_ref,
    more_ref,
    wide_ref,
    corner_ref,
):
    base = (1 - parity_ref[0]) * 8
    for p, (f, l) in enumerate(PLANES):
        rows = slice(ROW * p, ROW * p + ROW)
        wide_ref[f, 4 + l, 0:ROW, 0:COL] = block_ref[rows, :]
        wide_ref[f, base + l, 0:ROW, 0:COL] = pair_ref[rows, :]
    for f in range(2):
        for l in range(8):
            begin = (8 * f + l) * ROW
            wide_ref[4 + f, 2 + l, 0:ROW, 0:COL] = field_ref[begin : begin + ROW, :]
    place_sides(wide_ref, 4, east_ref[0:8, :], west_ref[0:8, :])
    for slot, begin in enumerate(FIELD_TILES):
        plane, row = divmod(begin, ROW)
        wide_ref[4 + plane // 8, 2 + plane % 8, row : row + 8, COL : 2 * COL] = beyond(
            east_ref[8:16, :], west_ref[8:16, :], slot
        )
    for side, ref in enumerate((before_ref, after_ref)):
        corners = ref[EDGE:, :]
        place_strip(
            wide_ref,
            4,
            side,
            STRIP,
            lambda f, l: 4,
            lambda at: ref[at : at + 1, :],
            corners,
            corner_ref,
        )
        for j in range(TALLY // 8, CORNERS):
            corner_ref[8 * j : 8 * j + 8, :] = turn(corners, -8 * j - 4, 1)
        for i in range(2):
            row = TALL - 1 - i if side == 0 else ROW + i
            for plane in range(16):
                at = TALLY + 16 * i + plane
                place = (4 + plane // 8, 2 + plane % 8, slice(row, row + 1))
                wide_ref[place + (slice(0, COL),)] = ref[at : at + 1, :]
                wide_ref[place + (slice(COL, 2 * COL),)] = corner_ref[at : at + 1, :]
    place_more(wide_ref, base, more_ref, corner_ref)


def step_kernel(
    parity_ref,
    given_ref,
    far_ref,
    outer_ref,
    state_ref,
    adjoint_ref,
    next_ref,
    wide_ref,
    first_ref,
    force_ref,
    back_ref,
    flat_ref,
    spread_ref,
    corner_ref,
):
    wide_ref[...] = given_ref[...]
    odd = parity_ref[0]
    for p, (f, l) in enumerate(PLANES):
        begin = pl.multiple_of(jnp.clip(ROW * p - (1 - odd) * (3 * ROW), 0, FAR - ROW), ROW)
        wide_ref[f, odd * 8 + l, 0:ROW, 0:COL] = far_ref[pl.ds(begin, ROW), :]
    place_more(wide_ref, odd * 8, far_ref.at[pl.ds(FAR, MORE)], corner_ref)

    def plus(x):
        return jnp.maximum(x, 0.0)

    def centre(level):
        return 1.0 - (
            jnp.abs(wide_ref[1, level]) + jnp.abs(wide_ref[2, level]) + jnp.abs(wide_ref[3, level])
        )

    def advance(get, level):
        here = get(level)
        c0, c1, c2 = (wide_ref[1 + k, level] for k in range(3))
        result = centre(level) * here
        result = result + plus(c0) * get(level - 1) + plus(-c0) * get(level + 1)
        result = result + plus(c1) * turn(here, 1, 0) + plus(-c1) * turn(here, -1, 0)
        return result + plus(c2) * turn(here, 1, 1) + plus(-c2) * turn(here, -1, 1)

    def retreat(get, level):
        here = get(level)
        c1, c2 = (wide_ref[2 + k, level] for k in range(2))
        result = centre(level) * here
        result = (
            result
            + plus(wide_ref[1, level + 1]) * get(level + 1)
            + plus(-wide_ref[1, level - 1]) * get(level - 1)
        )
        result = result + turn(plus(c1) * here, -1, 0) + turn(plus(-c1) * here, 1, 0)
        return result + turn(plus(c2) * here, -1, 1) + turn(plus(-c2) * here, 1, 1)

    for level in range(1, 11):
        first_ref[level] = advance(lambda l: wide_ref[0, l], level)
    for level in range(2, 10):
        state = advance(lambda l: first_ref[l], level)
        if 4 <= level < 8:
            state_ref[level - 4] = state[0:ROW, 0:COL]
        force_ref[level] = wide_ref[4, level] * state - wide_ref[5, level]
    for level in range(3, 9):
        back_ref[level] = retreat(lambda l: force_ref[l], level)
    for level in range(4, 8):
        result = retreat(lambda l: back_ref[l], level)[0:ROW, 0:COL]
        adjoint_ref[level - 4] = result
        flat_ref[ROW * (level - 4) : ROW * (level - 3), :] = result
    flat = flat_ref[...]
    high = flat.astype(BF16)
    rest = flat - high.astype(F32)
    middle = rest.astype(BF16)
    low = (rest - middle.astype(F32)).astype(BF16)
    table = column_table(COL * 4, COL, 1)
    spread = jnp.dot(high, table, preferred_element_type=F32)
    spread = spread + jnp.dot(middle, table, preferred_element_type=F32)
    spread = spread + jnp.dot(low, table, preferred_element_type=F32)
    for tile in range(4):
        cut = slice(COL * tile, COL * tile + COL)
        for part in range(4):
            spread_ref[pl.ds(part, LEV * ROW, stride=4), :] = spread[:, cut]
        outer = outer_ref[:, :, cut].astype(F32).reshape(LEV * ROW * 4, COL)
        result = (outer - spread_ref[...]).reshape(LEV, ROW * 4, COL)
        next_ref[:, :, cut] = result.astype(BF16)


def call(kernel, outs, ins, scratch=(), scalars=0, places={}, cost=500000, name=None):
    single = len(outs) == 1
    shapes = [jax.ShapeDtypeStruct(shape, kind) for shape, kind in outs]
    return pl.pallas_call(
        kernel,
        out_shape=shapes[0] if single else shapes,
        in_specs=[SMEM if i < scalars else places.get(i, VMEM) for i in range(len(ins))],
        out_specs=VMEM if single else [VMEM] * len(outs),
        scratch_shapes=list(scratch),
        compiler_params=pltpu.CompilerParams(vmem_limit_bytes=16 * 1024 * 1024),
        cost_estimate=pl.CostEstimate(flops=cost, bytes_accessed=cost, transcendentals=0),
        name=name,
    )(*ins)


def shift(size, by, wrap):
    return [
        (i, (i + by) % size) for i in range(size) if wrap or 0 <= i + by < size
    ]


def shards(outer_increment, courant, obs_column, obs_level, obs_value):
    lev = lax.axis_size("lev")
    lat_up, lat_down = (shift(lax.axis_size("lat"), by, False) for by in (1, -1))
    lon_up, lon_down = (shift(lax.axis_size("lon"), by, True) for by in (1, -1))
    pairs = [(i, i ^ 1) for i in range(lev)]
    far = [(i, i + 2) for i in range(0, lev - 2, 2)] + [(i, i - 2) for i in range(3, lev, 2)]
    position = lax.axis_index("lev").astype(jnp.int32)
    parity = (position & 1).reshape(1)
    lowest = (position * LEV).reshape(1)

    count = obs_column.shape[0]
    given = [outer_increment, courant]
    given += [array.reshape(1, count) for array in (obs_column, obs_level, obs_value)]
    block, fields, right, left = call(
        prepare_kernel,
        [((OWN, COL), F32), ((OWN, COL), F32), ((16, COL), F32), ((16, COL), F32)],
        [lowest] + [pltpu.with_memory_space_constraint(array, pltpu.HBM) for array in given],
        [pltpu.VMEM(array.shape, array.dtype) for array in given]
        + [pltpu.VMEM((LEV * ROW * 4, COL), F32), pltpu.SemaphoreType.DMA((5,))],
        scalars=1,
        places={i: HBM for i in range(1, 6)},
        name="prepare",
    )
    west = lax.ppermute(right, "lon", lon_up)
    east = lax.ppermute(left, "lon", lon_down)
    pair = lax.ppermute(block, "lev", pairs)
    up, down = call(
        strips_kernel,
        [((EDGE + 8, COL), F32), ((EDGE + 8, COL), F32)],
        [block, fields, west, east],
        [pltpu.VMEM((2 * OWN, COL), F32), pltpu.VMEM((EDGE, COL), F32)],
        cost=2000000000,
        name="strips",
    )
    before = lax.ppermute(up, "lat", lat_up)
    after = lax.ppermute(down, "lat", lat_down)
    joined = call(
        join_kernel,
        [((MORE, COL), F32)],
        [before, after, west, east],
        cost=1000,
        name="join",
    )
    more = lax.ppermute(joined, "lev", pairs)
    onward = call(
        forward_kernel, [((FAR + MORE, COL), F32)], [parity, pair, more], scalars=1, name="forward"
    )
    far_block = lax.ppermute(onward, "lev", far)
    tall = (DEEP, TALL, 2 * COL)
    wide = call(
        assemble_kernel,
        [((6,) + tall, F32)],
        [parity, block, fields, before, after, west, east, pair, more],
        [pltpu.VMEM((EDGE, COL), F32)],
        scalars=1,
        cost=1000000,
        name="assemble",
    )
    state, adjoint, outer_next = call(
        step_kernel,
        [
            ((LEV, ROW, COL), F32),
            ((LEV, ROW, COL), F32),
            (outer_increment.shape, BF16),
        ],
        [parity, wide, far_block, outer_increment],
        [
            pltpu.VMEM((6,) + tall, F32),
            pltpu.VMEM(tall, F32),
            pltpu.VMEM(tall, F32),
            pltpu.VMEM(tall, F32),
            pltpu.VMEM((LEV * ROW, COL), F32),
            pltpu.VMEM((LEV * ROW * 4, COL), F32),
            pltpu.VMEM((EDGE, COL), F32),
        ],
        scalars=1,
        name="steps",
    )
    return state, adjoint, outer_next


def solution(mesh):
    placed = (
        P("lev", "lat", "lon"),
        P(None, "lev", "lat", "lon"),
        P(("lat", "lon")),
        P(("lat", "lon")),
        P(("lat", "lon")),
    )
    return jax.shard_map(
        shards,
        mesh=mesh,
        in_specs=placed,
        out_specs=(P("lev", "lat", "lon"), P("lev", "lat", "lon"), P("lev", "lat", "lon")),
        check_vma=False,
    )
```

```python
import jax
import jax.numpy as jnp
from jax import lax
from jax.experimental import pallas as pl
from jax.experimental.pallas import tpu as pltpu
from jax.sharding import PartitionSpec as P

F32 = jnp.float32
BF16 = jnp.bfloat16
VMEM = pl.BlockSpec(memory_space=pltpu.VMEM)
SMEM = pl.BlockSpec(memory_space=pltpu.SMEM)

LEV = 4
ROW = 16
COL = 128
DEEP = 12
TALL = 24
ANY = pl.BlockSpec(memory_space=pl.ANY)
HBM = pl.BlockSpec(memory_space=pltpu.HBM)
PLANES = [(1, 0), (2, 0), (3, 0), (0, 0)]
PLANES += [(f, l) for l in (1, 2) for f in range(4)]
PLANES += [(0, 3), (1, 3), (2, 3), (3, 3)]
OWN = len(PLANES) * ROW
FAR = OWN - 3 * ROW


def reach(f, off):
    return max(0, (4 if f == 0 else 3) - off)


STRIP = [(p, i) for i in range(4) for p, (f, l) in enumerate(PLANES) if i < reach(f, 1 + min(l, 3 - l))]
NEAR = -(-len(STRIP) // 8) * 8
STRIP += [(p, i) for i in range(4) for p, (f, l) in enumerate(PLANES) if i < reach(f, 0) and (p, i) not in STRIP]
TALLY = -(-len(STRIP) // 8) * 8
EDGE = TALLY + 32


def column_table(wide, narrow, wide_axis):
    shape = (wide, narrow) if wide_axis == 0 else (narrow, wide)
    fine = lax.broadcasted_iota(jnp.int32, shape, wide_axis) >> 2
    coarse = lax.broadcasted_iota(jnp.int32, shape, 1 - wide_axis)
    return (fine == coarse).astype(F32).astype(BF16)


def prepare_kernel(
    lowest_ref,
    outer_hbm,
    courant_hbm,
    column_hbm,
    level_hbm,
    value_hbm,
    block_ref,
    field_ref,
    up_ref,
    down_ref,
    outer_ref,
    courant_ref,
    column_ref,
    level_ref,
    value_ref,
    sums_ref,
    sems,
):
    copies = [
        pltpu.make_async_copy(source, target, sems.at[i])
        for i, (source, target) in enumerate(
            (
                (outer_hbm, outer_ref),
                (courant_hbm, courant_ref),
                (column_hbm, column_ref),
                (level_hbm, level_ref),
                (value_hbm, value_ref),
            )
        )
    ]
    for copy in copies:
        copy.start()
    table = column_table(COL * 4, COL, 0)
    copies[1].wait()
    for p, (f, l) in enumerate(PLANES):
        if f > 0:
            block_ref[ROW * p : ROW * p + ROW, :] = courant_ref[f - 1, l].astype(F32)
    for i in (2, 3, 4):
        copies[i].wait()
    observe(lowest_ref[0], column_ref, level_ref, value_ref, field_ref)
    copies[0].wait()
    sums_ref[...] = jnp.dot(
        outer_ref[...].reshape(LEV * ROW * 4, COL * 4), table, preferred_element_type=F32
    )
    for p, (f, l) in enumerate(PLANES):
        if f == 0:
            total = sums_ref[pl.ds(ROW * 4 * l, ROW, stride=4), :]
            for part in range(1, 4):
                total = total + sums_ref[pl.ds(ROW * 4 * l + part, ROW, stride=4), :]
            block_ref[ROW * p : ROW * p + ROW, :] = total * 0.0625
    for ref, edge, step in ((up_ref, ROW - 1, -1), (down_ref, 0, 1)):
        for at, (p, i) in enumerate(STRIP):
            row = ROW * p + edge + step * i
            ref[at : at + 1, :] = block_ref[row : row + 1, :]
        ref[len(STRIP) : TALLY, :] = jnp.zeros((TALLY - len(STRIP), COL), F32)
        for i in range(2):
            begin = TALLY + 16 * i
            ref[begin : begin + 16, :] = field_ref[pl.ds(edge + step * i, 16, stride=ROW), :]


def observe(lowest, column_ref, level_ref, value_ref, field_ref):
    count = column_ref.shape[1]
    chunk = 512
    total = jnp.zeros((4 * COL, COL), F32)
    for begin in range(0, count, chunk):
        cut = slice(begin, begin + chunk)
        cell = column_ref[:, cut]
        place = (level_ref[:, cut] - lowest + 2) * ROW + (cell >> 7)
        value = value_ref[:, cut]
        high = value.astype(BF16).astype(F32)
        rest = value - high
        middle = rest.astype(BF16).astype(F32)
        low = rest - middle
        index = lax.broadcasted_iota(jnp.int32, (COL, chunk), 0)
        here = index == place
        across = jnp.where(index == (cell & 127), 1.0, 0.0).astype(BF16)
        down = jnp.concatenate(
            [jnp.where(here, part, 0.0).astype(BF16) for part in (1.0, high, middle, low)], axis=0
        )
        total = total + lax.dot_general(
            down, across, (((1,), (1,)), ((), ())), preferred_element_type=F32
        )
    field_ref[0:128, :] = total[0:128]
    field_ref[128:256, :] = (total[128:256] + total[256:384]) + total[384:512]


def tile_table():
    own = [(f, l, part) for f in range(4) for l in range(LEV) for part in range(3)]
    first = [(f, l, part) for f, l, part in own if part < 2 or reach(f, 1 + min(l, 3 - l)) > 1]
    tiles = first + [tile for tile in own if tile not in first]
    for f in (4, 5):
        for l in range(1, 7):
            tiles += [(f, l, part) for part in range(3 if 2 <= l < 6 else 2)]
    return tiles, len(first)


TILES, SENT_ON = tile_table()
PACKS = -(-len(TILES) // 32) * 8
ON = -(-SENT_ON // 32) * 8
MORE = 2 * NEAR + 2 * ON


def edges_kernel(block_ref, field_ref, before_ref, after_ref, own_ref, obs_ref, near_ref, right_ref, left_ref):
    for p, (f, l) in enumerate(PLANES):
        own_ref[f, l, 0:ROW, :] = block_ref[ROW * p : ROW * p + ROW, :]
    for f in range(2):
        for l in range(8):
            begin = (f * 8 + l) * ROW
            obs_ref[f, l, 0:ROW, :] = field_ref[begin : begin + ROW, :]
    for side, ref in enumerate((before_ref, after_ref)):
        near_ref[NEAR * side : NEAR * side + NEAR, :] = ref[0:NEAR, :]
        for at, (p, i) in enumerate(STRIP):
            f, l = PLANES[p]
            row = TALL - 1 - i if side == 0 else ROW + i
            own_ref[f, l, row : row + 1, :] = ref[at : at + 1, :]
        for i in range(2):
            row = TALL - 1 - i if side == 0 else ROW + i
            for plane in range(16):
                at = TALLY + 16 * i + plane
                obs_ref[plane // 8, plane % 8, row : row + 1, :] = ref[at : at + 1, :]
    group = lax.broadcasted_iota(jnp.int32, (8, COL), 1) >> 2
    for pack in range(0, PACKS, 8):
        right = jnp.zeros((8, COL), F32)
        left = jnp.zeros((8, COL), F32)
        for slot, (f, l, part) in enumerate(TILES[4 * pack : 4 * pack + 32]):
            ref, f = (own_ref, f) if f < 4 else (obs_ref, f - 4)
            tile = ref[f, l, 8 * part : 8 * part + 8, :]
            right = jnp.where(group == slot, turn(tile, 4 * slot + 4, 1), right)
            left = jnp.where(group == slot, turn(tile, 4 * slot, 1), left)
        right_ref[pack : pack + 8, :] = right
        left_ref[pack : pack + 8, :] = left


def turn(tile, shift, axis):
    shift = shift % tile.shape[axis]
    return pltpu.roll(tile, shift, axis) if shift else tile


def join_kernel(near_ref, west_ref, east_ref, more_ref):
    more_ref[0 : 2 * NEAR, :] = near_ref[...]
    more_ref[2 * NEAR : 2 * NEAR + ON, :] = west_ref[0:ON, :]
    more_ref[2 * NEAR + ON : MORE, :] = east_ref[0:ON, :]


def forward_kernel(parity_ref, pair_ref, later_ref, far_ref):
    del later_ref
    begin = pl.multiple_of((1 - parity_ref[0]) * (3 * ROW), ROW)
    far_ref[...] = pair_ref[pl.ds(begin, FAR), :]


def place_strips(wide_ref, base, ref, start):
    for side in range(2):
        for at, (p, i) in enumerate(STRIP[:NEAR]):
            f, l = PLANES[p]
            if i < reach(f, 1 + min(l, 3 - l)):
                row = TALL - 1 - i if side == 0 else ROW + i
                at += start + NEAR * side
                wide_ref[f, base + l, row : row + 1, 0:COL] = ref[at : at + 1, :]


def place_edges(wide_ref, base, tiles, west, east):
    half = lax.broadcasted_iota(jnp.int32, (8, COL), 1) < 64
    for slot, (f, l, part) in enumerate(tiles):
        pack, lane = divmod(slot, 32)
        level = base + l if f < 4 else 2 + l
        wide_ref[f, level, 8 * part : 8 * part + 8, COL : 2 * COL] = jnp.where(
            half, turn(east(8 * pack), -4 * lane, 1), turn(west(8 * pack), -4 * lane - 4, 1)
        )


def place_more(wide_ref, base, ref, start):
    place_strips(wide_ref, base, ref, start)
    west = start + 2 * NEAR
    place_edges(
        wide_ref,
        base,
        TILES[:SENT_ON],
        lambda row: ref[west + row : west + row + 8, :],
        lambda row: ref[west + ON + row : west + ON + row + 8, :],
    )


def assemble_kernel(parity_ref, own_ref, obs_ref, west_ref, east_ref, pair_ref, more_ref, wide_ref):
    wide_ref[0:4, 4:8, :, 0:COL] = own_ref[...]
    wide_ref[4:6, 2:10, :, 0:COL] = obs_ref[...]
    place_edges(
        wide_ref,
        4,
        TILES,
        lambda row: west_ref[row : row + 8, :],
        lambda row: east_ref[row : row + 8, :],
    )
    base = (1 - parity_ref[0]) * 8
    for p, (f, l) in enumerate(PLANES):
        wide_ref[f, base + l, 0:ROW, 0:COL] = pair_ref[ROW * p : ROW * p + ROW, :]
    place_more(wide_ref, base, more_ref, 0)


def step_kernel(
    parity_ref,
    given_ref,
    far_ref,
    far_more_ref,
    outer_ref,
    state_ref,
    adjoint_ref,
    next_ref,
    wide_ref,
    first_ref,
    force_ref,
    back_ref,
    flat_ref,
    spread_ref,
):
    wide_ref[...] = given_ref[0:4]
    odd = parity_ref[0]
    for p, (f, l) in enumerate(PLANES):
        begin = pl.multiple_of(jnp.clip(ROW * p - (1 - odd) * (3 * ROW), 0, FAR - ROW), ROW)
        wide_ref[f, odd * 8 + l, 0:ROW, 0:COL] = far_ref[pl.ds(begin, ROW), :]
    place_more(wide_ref, odd * 8, far_more_ref, 0)

    def plus(x):
        return jnp.maximum(x, 0.0)

    def centre(level):
        return 1.0 - (
            jnp.abs(wide_ref[1, level]) + jnp.abs(wide_ref[2, level]) + jnp.abs(wide_ref[3, level])
        )

    def advance(get, level):
        here = get(level)
        c0, c1, c2 = (wide_ref[1 + k, level] for k in range(3))
        result = centre(level) * here
        result = result + plus(c0) * get(level - 1) + plus(-c0) * get(level + 1)
        result = result + plus(c1) * turn(here, 1, 0) + plus(-c1) * turn(here, -1, 0)
        return result + plus(c2) * turn(here, 1, 1) + plus(-c2) * turn(here, -1, 1)

    def retreat(get, level):
        here = get(level)
        c1, c2 = (wide_ref[2 + k, level] for k in range(2))
        result = centre(level) * here
        result = (
            result
            + plus(wide_ref[1, level + 1]) * get(level + 1)
            + plus(-wide_ref[1, level - 1]) * get(level - 1)
        )
        result = result + turn(plus(c1) * here, -1, 0) + turn(plus(-c1) * here, 1, 0)
        return result + turn(plus(c2) * here, -1, 1) + turn(plus(-c2) * here, 1, 1)

    for level in range(1, 11):
        first_ref[level] = advance(lambda l: wide_ref[0, l], level)
    for level in range(2, 10):
        state = advance(lambda l: first_ref[l], level)
        if 4 <= level < 8:
            state_ref[level - 4] = state[0:ROW, 0:COL]
        force_ref[level] = given_ref[4, level] * state - given_ref[5, level]
    for level in range(3, 9):
        back_ref[level] = retreat(lambda l: force_ref[l], level)
    for level in range(4, 8):
        result = retreat(lambda l: back_ref[l], level)[0:ROW, 0:COL]
        adjoint_ref[level - 4] = result
        flat_ref[ROW * (level - 4) : ROW * (level - 3), :] = result
    flat = flat_ref[...]
    high = flat.astype(BF16)
    rest = flat - high.astype(F32)
    middle = rest.astype(BF16)
    low = (rest - middle.astype(F32)).astype(BF16)
    table = column_table(COL * 4, COL, 1)
    spread = jnp.dot(high, table, preferred_element_type=F32)
    spread = spread + jnp.dot(middle, table, preferred_element_type=F32)
    spread = spread + jnp.dot(low, table, preferred_element_type=F32)
    for tile in range(4):
        cut = slice(COL * tile, COL * tile + COL)
        for part in range(4):
            spread_ref[pl.ds(part, LEV * ROW, stride=4), :] = spread[:, cut]
        outer = outer_ref[:, :, cut].astype(F32).reshape(LEV * ROW * 4, COL)
        result = (outer - spread_ref[...]).reshape(LEV, ROW * 4, COL)
        next_ref[:, :, cut] = result.astype(BF16)


def call(kernel, outs, ins, scratch=(), scalars=0, places={}, cost=500000, name=None):
    single = len(outs) == 1
    shapes = [jax.ShapeDtypeStruct(shape, kind) for shape, kind in outs]
    return pl.pallas_call(
        kernel,
        out_shape=shapes[0] if single else shapes,
        in_specs=[SMEM if i < scalars else places.get(i, VMEM) for i in range(len(ins))],
        out_specs=VMEM if single else [VMEM] * len(outs),
        scratch_shapes=list(scratch),
        compiler_params=pltpu.CompilerParams(vmem_limit_bytes=16 * 1024 * 1024),
        cost_estimate=pl.CostEstimate(flops=cost, bytes_accessed=cost, transcendentals=0),
        name=name,
    )(*ins)


def shift(size, by, wrap):
    return [
        (i, (i + by) % size) for i in range(size) if wrap or 0 <= i + by < size
    ]


def shards(outer_increment, courant, obs_column, obs_level, obs_value):
    lev = lax.axis_size("lev")
    lat_up, lat_down = (shift(lax.axis_size("lat"), by, False) for by in (1, -1))
    lon_up, lon_down = (shift(lax.axis_size("lon"), by, True) for by in (1, -1))
    pairs = [(i, i ^ 1) for i in range(lev)]
    far = [(i, i + 2) for i in range(0, lev - 2, 2)] + [(i, i - 2) for i in range(3, lev, 2)]
    position = lax.axis_index("lev").astype(jnp.int32)
    parity = (position & 1).reshape(1)
    lowest = (position * LEV).reshape(1)

    count = obs_column.shape[0]
    given = [outer_increment, courant]
    given += [array.reshape(1, count) for array in (obs_column, obs_level, obs_value)]
    block, fields, up, down = call(
        prepare_kernel,
        [((OWN, COL), F32), ((OWN, COL), F32), ((EDGE, COL), F32), ((EDGE, COL), F32)],
        [lowest] + [pltpu.with_memory_space_constraint(array, pltpu.HBM) for array in given],
        [pltpu.VMEM(array.shape, array.dtype) for array in given]
        + [pltpu.VMEM((LEV * ROW * 4, COL), F32), pltpu.SemaphoreType.DMA((5,))],
        scalars=1,
        places={i: HBM for i in range(1, 6)},
        name="prepare",
    )
    before = lax.ppermute(up, "lat", lat_up)
    after = lax.ppermute(down, "lat", lat_down)
    pair = lax.ppermute(block, "lev", pairs)
    own, obs, near, right, left = call(
        edges_kernel,
        [
            ((4, LEV, TALL, COL), F32),
            ((2, 8, TALL, COL), F32),
            ((2 * NEAR, COL), F32),
            ((PACKS, COL), F32),
            ((PACKS, COL), F32),
        ],
        [block, fields, before, after],
        cost=2000000000, name="edges",
    )
    west = lax.ppermute(right, "lon", lon_up)
    east = lax.ppermute(left, "lon", lon_down)
    joined = call(join_kernel, [((MORE, COL), F32)], [near, west, east], cost=1000, name="join")
    more = lax.ppermute(joined, "lev", pairs)
    onward = call(
        forward_kernel,
        [((FAR, COL), F32)],
        [parity, pair, joined],
        scalars=1,
        places={2: ANY},
        cost=1000, name="forward",
    )
    far_block = lax.ppermute(onward, "lev", far)
    far_more = lax.ppermute(more, "lev", far)
    tall = (DEEP, TALL, 2 * COL)
    wide = call(
        assemble_kernel,
        [((6,) + tall, F32)],
        [parity, own, obs, west, east, pair, more],
        scalars=1,
        cost=1000000000, name="assemble",
    )
    state, adjoint, outer_next = call(
        step_kernel,
        [
            ((LEV, ROW, COL), F32),
            ((LEV, ROW, COL), F32),
            (outer_increment.shape, BF16),
        ],
        [parity, wide, far_block, far_more, outer_increment],
        [
            pltpu.VMEM((4,) + tall, F32),
            pltpu.VMEM(tall, F32),
            pltpu.VMEM(tall, F32),
            pltpu.VMEM(tall, F32),
            pltpu.VMEM((LEV * ROW, COL), F32),
            pltpu.VMEM((LEV * ROW * 4, COL), F32),
        ],
        scalars=1,
        name="steps",
    )
    return state, adjoint, outer_next


def solution(mesh):
    placed = (
        P("lev", "lat", "lon"),
        P(None, "lev", "lat", "lon"),
        P(("lat", "lon")),
        P(("lat", "lon")),
        P(("lat", "lon")),
    )
    return jax.shard_map(
        shards,
        mesh=mesh,
        in_specs=placed,
        out_specs=(P("lev", "lat", "lon"), P("lev", "lat", "lon"), P("lev", "lat", "lon")),
        check_vma=False,
    )
```

```python
import jax
import jax.numpy as jnp
from jax import lax
from jax.experimental import pallas as pl
from jax.experimental.pallas import tpu as pltpu
from jax.sharding import PartitionSpec as P

F32 = jnp.float32
BF16 = jnp.bfloat16
VMEM = pl.BlockSpec(memory_space=pltpu.VMEM)
SMEM = pl.BlockSpec(memory_space=pltpu.SMEM)

LEV = 4
ROW = 16
COL = 128
DEEP = 12
TALL = 24
ANY = pl.BlockSpec(memory_space=pl.ANY)
HBM = pl.BlockSpec(memory_space=pltpu.HBM)
PLANES = [(1, 0), (2, 0), (3, 0), (0, 0)]
PLANES += [(f, l) for l in (1, 2) for f in range(4)]
PLANES += [(0, 3), (1, 3), (2, 3), (3, 3)]
OWN = len(PLANES) * ROW
FAR = OWN - 3 * ROW


def reach(f, off):
    return max(0, (4 if f == 0 else 3) - off)


STRIP = [(p, i) for i in range(4) for p, (f, l) in enumerate(PLANES) if i < reach(f, 1 + min(l, 3 - l))]
NEAR = -(-len(STRIP) // 8) * 8
STRIP += [(p, i) for i in range(4) for p, (f, l) in enumerate(PLANES) if i < reach(f, 0) and (p, i) not in STRIP]
TALLY = -(-len(STRIP) // 8) * 8
EDGE = TALLY + 32


def column_table(wide, narrow, wide_axis):
    shape = (wide, narrow) if wide_axis == 0 else (narrow, wide)
    fine = lax.broadcasted_iota(jnp.int32, shape, wide_axis) >> 2
    coarse = lax.broadcasted_iota(jnp.int32, shape, 1 - wide_axis)
    return (fine == coarse).astype(F32).astype(BF16)


def prepare_kernel(
    lowest_ref,
    outer_hbm,
    courant_hbm,
    column_hbm,
    level_hbm,
    value_hbm,
    block_ref,
    field_ref,
    up_ref,
    down_ref,
    outer_ref,
    courant_ref,
    column_ref,
    level_ref,
    value_ref,
    sums_ref,
    sems,
):
    copies = [
        pltpu.make_async_copy(source, target, sems.at[i])
        for i, (source, target) in enumerate(
            (
                (outer_hbm, outer_ref),
                (courant_hbm, courant_ref),
                (column_hbm, column_ref),
                (level_hbm, level_ref),
                (value_hbm, value_ref),
            )
        )
    ]
    for copy in copies:
        copy.start()
    table = column_table(COL * 4, COL, 0)
    copies[1].wait()
    for p, (f, l) in enumerate(PLANES):
        if f > 0:
            block_ref[ROW * p : ROW * p + ROW, :] = courant_ref[f - 1, l].astype(F32)
    for i in (2, 3, 4):
        copies[i].wait()
    observe(lowest_ref[0], column_ref, level_ref, value_ref, field_ref)
    copies[0].wait()
    sums_ref[...] = jnp.dot(
        outer_ref[...].reshape(LEV * ROW * 4, COL * 4), table, preferred_element_type=F32
    )
    for p, (f, l) in enumerate(PLANES):
        if f == 0:
            total = sums_ref[pl.ds(ROW * 4 * l, ROW, stride=4), :]
            for part in range(1, 4):
                total = total + sums_ref[pl.ds(ROW * 4 * l + part, ROW, stride=4), :]
            block_ref[ROW * p : ROW * p + ROW, :] = total * 0.0625
    for ref, edge, step in ((up_ref, ROW - 1, -1), (down_ref, 0, 1)):
        for at, (p, i) in enumerate(STRIP):
            row = ROW * p + edge + step * i
            ref[at : at + 1, :] = block_ref[row : row + 1, :]
        ref[len(STRIP) : TALLY, :] = jnp.zeros((TALLY - len(STRIP), COL), F32)
        for i in range(2):
            begin = TALLY + 16 * i
            ref[begin : begin + 16, :] = field_ref[pl.ds(edge + step * i, 16, stride=ROW), :]


def observe(lowest, column_ref, level_ref, value_ref, field_ref):
    count = column_ref.shape[1]
    chunk = 512
    total = jnp.zeros((4 * COL, COL), F32)
    for begin in range(0, count, chunk):
        cut = slice(begin, begin + chunk)
        cell = column_ref[:, cut]
        place = (level_ref[:, cut] - lowest + 2) * ROW + (cell >> 7)
        value = value_ref[:, cut]
        high = value.astype(BF16).astype(F32)
        rest = value - high
        middle = rest.astype(BF16).astype(F32)
        low = rest - middle
        index = lax.broadcasted_iota(jnp.int32, (COL, chunk), 0)
        here = index == place
        across = jnp.where(index == (cell & 127), 1.0, 0.0).astype(BF16)
        down = jnp.concatenate(
            [jnp.where(here, part, 0.0).astype(BF16) for part in (1.0, high, middle, low)], axis=0
        )
        total = total + lax.dot_general(
            down, across, (((1,), (1,)), ((), ())), preferred_element_type=F32
        )
    field_ref[0:128, :] = total[0:128]
    field_ref[128:256, :] = (total[128:256] + total[256:384]) + total[384:512]


def tile_table():
    own = [(f, l, part) for f in range(4) for l in range(LEV) for part in range(3)]
    first = [(f, l, part) for f, l, part in own if part < 2 or reach(f, 1 + min(l, 3 - l)) > 1]
    tiles = first + [tile for tile in own if tile not in first]
    for f in (4, 5):
        for l in range(1, 7):
            tiles += [(f, l, part) for part in range(3 if 2 <= l < 6 else 2)]
    return tiles, len(first)


TILES, SENT_ON = tile_table()
PACKS = -(-len(TILES) // 32) * 8
ON = -(-SENT_ON // 32) * 8
MORE = 2 * NEAR + 2 * ON


def edges_kernel(block_ref, field_ref, before_ref, after_ref, own_ref, obs_ref, near_ref, right_ref, left_ref):
    for p, (f, l) in enumerate(PLANES):
        own_ref[f, l, 0:ROW, :] = block_ref[ROW * p : ROW * p + ROW, :]
    for f in range(2):
        for l in range(8):
            begin = (f * 8 + l) * ROW
            obs_ref[f, l, 0:ROW, :] = field_ref[begin : begin + ROW, :]
    for side, ref in enumerate((before_ref, after_ref)):
        near_ref[NEAR * side : NEAR * side + NEAR, :] = ref[0:NEAR, :]
        for at, (p, i) in enumerate(STRIP):
            f, l = PLANES[p]
            row = TALL - 1 - i if side == 0 else ROW + i
            own_ref[f, l, row : row + 1, :] = ref[at : at + 1, :]
        for i in range(2):
            row = TALL - 1 - i if side == 0 else ROW + i
            for plane in range(16):
                at = TALLY + 16 * i + plane
                obs_ref[plane // 8, plane % 8, row : row + 1, :] = ref[at : at + 1, :]
    group = lax.broadcasted_iota(jnp.int32, (8, COL), 1) >> 2
    for pack in range(0, PACKS, 8):
        right = jnp.zeros((8, COL), F32)
        left = jnp.zeros((8, COL), F32)
        for slot, (f, l, part) in enumerate(TILES[4 * pack : 4 * pack + 32]):
            ref, f = (own_ref, f) if f < 4 else (obs_ref, f - 4)
            tile = ref[f, l, 8 * part : 8 * part + 8, :]
            right = jnp.where(group == slot, turn(tile, 4 * slot + 4, 1), right)
            left = jnp.where(group == slot, turn(tile, 4 * slot, 1), left)
        right_ref[pack : pack + 8, :] = right
        left_ref[pack : pack + 8, :] = left


def turn(tile, shift, axis):
    shift = shift % tile.shape[axis]
    return pltpu.roll(tile, shift, axis) if shift else tile


def join_kernel(near_ref, west_ref, east_ref, more_ref):
    more_ref[0 : 2 * NEAR, :] = near_ref[...]
    more_ref[2 * NEAR : 2 * NEAR + ON, :] = west_ref[0:ON, :]
    more_ref[2 * NEAR + ON : MORE, :] = east_ref[0:ON, :]


def forward_kernel(parity_ref, pair_ref, later_ref, far_ref):
    del later_ref
    begin = pl.multiple_of((1 - parity_ref[0]) * (3 * ROW), ROW)
    far_ref[...] = pair_ref[pl.ds(begin, FAR), :]


def place_strips(wide_ref, base, ref, start):
    for side in range(2):
        for at, (p, i) in enumerate(STRIP[:NEAR]):
            f, l = PLANES[p]
            if i < reach(f, 1 + min(l, 3 - l)):
                row = TALL - 1 - i if side == 0 else ROW + i
                at += start + NEAR * side
                wide_ref[f, base + l, row : row + 1, 0:COL] = ref[at : at + 1, :]


def place_edges(wide_ref, base, tiles, west, east):
    half = lax.broadcasted_iota(jnp.int32, (8, COL), 1) < 64
    for slot, (f, l, part) in enumerate(tiles):
        pack, lane = divmod(slot, 32)
        level = base + l if f < 4 else 2 + l
        wide_ref[f, level, 8 * part : 8 * part + 8, COL : 2 * COL] = jnp.where(
            half, turn(east(8 * pack), -4 * lane, 1), turn(west(8 * pack), -4 * lane - 4, 1)
        )


def place_more(wide_ref, base, ref, start):
    place_strips(wide_ref, base, ref, start)
    west = start + 2 * NEAR
    place_edges(
        wide_ref,
        base,
        TILES[:SENT_ON],
        lambda row: ref[west + row : west + row + 8, :],
        lambda row: ref[west + ON + row : west + ON + row + 8, :],
    )


def assemble_kernel(
    parity_ref,
    own_ref,
    obs_ref,
    west_ref,
    east_ref,
    pair_ref,
    more_ref,
    wide_ref,
    near_first_ref,
    near_force_ref,
    near_back_ref,
    near_state_ref,
    first_ref,
    force_ref,
):
    wide_ref[0:4, 4:8, :, 0:COL] = own_ref[...]
    wide_ref[4:6, 2:10, :, 0:COL] = obs_ref[...]
    place_edges(
        wide_ref,
        4,
        TILES,
        lambda row: west_ref[row : row + 8, :],
        lambda row: east_ref[row : row + 8, :],
    )
    base = (1 - parity_ref[0]) * 8
    for p, (f, l) in enumerate(PLANES):
        wide_ref[f, base + l, 0:ROW, 0:COL] = pair_ref[ROW * p : ROW * p + ROW, :]
    place_more(wide_ref, base, more_ref, 0)
    parity = parity_ref[0]
    odd = parity == 1

    def field(f, j):
        return wide_ref[f, level_of(parity, j)]

    for j in range(5, 11):
        first_ref[j] = advance(odd, field, lambda i: field(0, i), j)
    for j in range(6, 10):
        state = advance(odd, field, lambda i: first_ref[i], j)
        if j < 8:
            near_state_ref[j - 6] = state[0:ROW, 0:COL]
        force_ref[j] = field(4, j) * state - field(5, j)
    for j in range(7, 9):
        near_back_ref[j - 7] = retreat(odd, field, lambda i: force_ref[i], j)
    near_first_ref[...] = first_ref[5:7]
    near_force_ref[...] = force_ref[6:8]


def plus(x):
    return jnp.maximum(x, 0.0)


def centre(field, j):
    return 1.0 - (jnp.abs(field(1, j)) + jnp.abs(field(2, j)) + jnp.abs(field(3, j)))


def advance(odd, field, get, j):
    here = get(j)
    below, above = jnp.where(odd, get(j + 1), get(j - 1)), jnp.where(odd, get(j - 1), get(j + 1))
    c0, c1, c2 = (field(1 + k, j) for k in range(3))
    result = centre(field, j) * here
    result = result + plus(c0) * below + plus(-c0) * above
    result = result + plus(c1) * turn(here, 1, 0) + plus(-c1) * turn(here, -1, 0)
    return result + plus(c2) * turn(here, 1, 1) + plus(-c2) * turn(here, -1, 1)


def retreat(odd, field, get, j):
    here = get(j)
    sign = jnp.where(odd, -1.0, 1.0)
    c1, c2 = field(2, j), field(3, j)
    result = centre(field, j) * here
    result = result + plus(sign * field(1, j + 1)) * get(j + 1) + plus(-sign * field(1, j - 1)) * get(j - 1)
    result = result + turn(plus(c1) * here, -1, 0) + turn(plus(-c1) * here, 1, 0)
    return result + turn(plus(c2) * here, -1, 1) + turn(plus(-c2) * here, 1, 1)


def level_of(odd, j):
    return j + odd * (11 - 2 * j)


def step_kernel(
    parity_ref,
    given_ref,
    given_first_ref,
    given_force_ref,
    given_back_ref,
    given_state_ref,
    far_ref,
    far_more_ref,
    outer_ref,
    state_ref,
    adjoint_ref,
    next_ref,
    wide_ref,
    first_ref,
    force_ref,
    back_ref,
    flat_ref,
    spread_ref,
):
    parity = parity_ref[0]
    odd = parity == 1
    for p, (f, l) in enumerate(PLANES):
        begin = pl.multiple_of(jnp.clip(ROW * p - (1 - parity) * (3 * ROW), 0, FAR - ROW), ROW)
        wide_ref[f, l, 0:ROW, 0:COL] = far_ref[pl.ds(begin, ROW), :]
    place_more(wide_ref, 0, far_more_ref, 0)

    def field(f, j):
        return wide_ref[f, j + parity * (3 - 2 * j)] if j < 4 else given_ref[f, level_of(parity, j)]

    first_ref[5:7] = given_first_ref[...]
    force_ref[6:8] = given_force_ref[...]
    back_ref[7:9] = given_back_ref[...]
    for j in (6, 7):
        state_ref[level_of(parity, j) - 4] = given_state_ref[j - 6]
    for j in range(1, 5):
        first_ref[j] = advance(odd, field, lambda i: field(0, i), j)
    for j in range(2, 6):
        state = advance(odd, field, lambda i: first_ref[i], j)
        if j >= 4:
            state_ref[level_of(parity, j) - 4] = state[0:ROW, 0:COL]
        level = level_of(parity, j)
        force_ref[j] = given_ref[4, level] * state - given_ref[5, level]
    for j in range(3, 7):
        back_ref[j] = retreat(odd, field, lambda i: force_ref[i], j)
    for j in range(4, 8):
        result = retreat(odd, field, lambda i: back_ref[i], j)[0:ROW, 0:COL]
        place = level_of(parity, j) - 4
        adjoint_ref[place] = result
        flat_ref[pl.ds(pl.multiple_of(place * ROW, ROW), ROW), :] = result
    flat = flat_ref[...]
    high = flat.astype(BF16)
    rest = flat - high.astype(F32)
    middle = rest.astype(BF16)
    low = (rest - middle.astype(F32)).astype(BF16)
    table = column_table(COL * 4, COL, 1)
    spread = jnp.dot(high, table, preferred_element_type=F32)
    spread = spread + jnp.dot(middle, table, preferred_element_type=F32)
    spread = spread + jnp.dot(low, table, preferred_element_type=F32)
    for tile in range(4):
        cut = slice(COL * tile, COL * tile + COL)
        for part in range(4):
            spread_ref[pl.ds(part, LEV * ROW, stride=4), :] = spread[:, cut]
        outer = outer_ref[:, :, cut].astype(F32).reshape(LEV * ROW * 4, COL)
        result = (outer - spread_ref[...]).reshape(LEV, ROW * 4, COL)
        next_ref[:, :, cut] = result.astype(BF16)


def call(kernel, outs, ins, scratch=(), scalars=0, places={}, cost=500000, name=None):
    single = len(outs) == 1
    shapes = [jax.ShapeDtypeStruct(shape, kind) for shape, kind in outs]
    return pl.pallas_call(
        kernel,
        out_shape=shapes[0] if single else shapes,
        in_specs=[SMEM if i < scalars else places.get(i, VMEM) for i in range(len(ins))],
        out_specs=VMEM if single else [VMEM] * len(outs),
        scratch_shapes=list(scratch),
        compiler_params=pltpu.CompilerParams(vmem_limit_bytes=16 * 1024 * 1024),
        cost_estimate=pl.CostEstimate(flops=cost, bytes_accessed=cost, transcendentals=0),
        name=name,
    )(*ins)


def shift(size, by, wrap):
    return [
        (i, (i + by) % size) for i in range(size) if wrap or 0 <= i + by < size
    ]


def shards(outer_increment, courant, obs_column, obs_level, obs_value):
    lev = lax.axis_size("lev")
    lat_up, lat_down = (shift(lax.axis_size("lat"), by, False) for by in (1, -1))
    lon_up, lon_down = (shift(lax.axis_size("lon"), by, True) for by in (1, -1))
    pairs = [(i, i ^ 1) for i in range(lev)]
    far = [(i, i + 2) for i in range(0, lev - 2, 2)] + [(i, i - 2) for i in range(3, lev, 2)]
    position = lax.axis_index("lev").astype(jnp.int32)
    parity = (position & 1).reshape(1)
    lowest = (position * LEV).reshape(1)

    count = obs_column.shape[0]
    given = [outer_increment, courant]
    given += [array.reshape(1, count) for array in (obs_column, obs_level, obs_value)]
    block, fields, up, down = call(
        prepare_kernel,
        [((OWN, COL), F32), ((OWN, COL), F32), ((EDGE, COL), F32), ((EDGE, COL), F32)],
        [lowest] + [pltpu.with_memory_space_constraint(array, pltpu.HBM) for array in given],
        [pltpu.VMEM(array.shape, array.dtype) for array in given]
        + [pltpu.VMEM((LEV * ROW * 4, COL), F32), pltpu.SemaphoreType.DMA((5,))],
        scalars=1,
        places={i: HBM for i in range(1, 6)},
        name="prepare",
    )
    before = lax.ppermute(up, "lat", lat_up)
    after = lax.ppermute(down, "lat", lat_down)
    pair = lax.ppermute(block, "lev", pairs)
    own, obs, near, right, left = call(
        edges_kernel,
        [
            ((4, LEV, TALL, COL), F32),
            ((2, 8, TALL, COL), F32),
            ((2 * NEAR, COL), F32),
            ((PACKS, COL), F32),
            ((PACKS, COL), F32),
        ],
        [block, fields, before, after],
        cost=2000000000, name="edges",
    )
    west = lax.ppermute(right, "lon", lon_up)
    east = lax.ppermute(left, "lon", lon_down)
    joined = call(join_kernel, [((MORE, COL), F32)], [near, west, east], cost=1000, name="join")
    more = lax.ppermute(joined, "lev", pairs)
    onward = call(
        forward_kernel,
        [((FAR, COL), F32)],
        [parity, pair, joined],
        scalars=1,
        places={2: ANY},
        cost=1000, name="forward",
    )
    far_block = lax.ppermute(onward, "lev", far)
    far_more = lax.ppermute(more, "lev", far)
    tall = (DEEP, TALL, 2 * COL)
    plane = (TALL, 2 * COL)
    near = call(
        assemble_kernel,
        [
            ((6,) + tall, F32),
            ((2,) + plane, F32),
            ((2,) + plane, F32),
            ((2,) + plane, F32),
            ((2, ROW, COL), F32),
        ],
        [parity, own, obs, west, east, pair, more],
        [pltpu.VMEM(tall, F32), pltpu.VMEM(tall, F32)],
        scalars=1,
        cost=1000000000,
        name="assemble",
    )
    state, adjoint, outer_next = call(
        step_kernel,
        [
            ((LEV, ROW, COL), F32),
            ((LEV, ROW, COL), F32),
            (outer_increment.shape, BF16),
        ],
        [parity, *near, far_block, far_more, outer_increment],
        [
            pltpu.VMEM((4, LEV) + plane, F32),
            pltpu.VMEM(tall, F32),
            pltpu.VMEM(tall, F32),
            pltpu.VMEM(tall, F32),
            pltpu.VMEM((LEV * ROW, COL), F32),
            pltpu.VMEM((LEV * ROW * 4, COL), F32),
        ],
        scalars=1,
        name="steps",
    )
    return state, adjoint, outer_next


def solution(mesh):
    placed = (
        P("lev", "lat", "lon"),
        P(None, "lev", "lat", "lon"),
        P(("lat", "lon")),
        P(("lat", "lon")),
        P(("lat", "lon")),
    )
    return jax.shard_map(
        shards,
        mesh=mesh,
        in_specs=placed,
        out_specs=(P("lev", "lat", "lon"), P("lev", "lat", "lon"), P("lev", "lat", "lon")),
        check_vma=False,
    )
```

```python
import jax
import jax.numpy as jnp
from jax import lax
from jax.experimental import pallas as pl
from jax.experimental.pallas import tpu as pltpu
from jax.sharding import PartitionSpec as P

F32 = jnp.float32
BF16 = jnp.bfloat16
VMEM = pl.BlockSpec(memory_space=pltpu.VMEM)
SMEM = pl.BlockSpec(memory_space=pltpu.SMEM)

LEV = 4
ROW = 16
COL = 128
DEEP = 12
TALL = 24
ANY = pl.BlockSpec(memory_space=pl.ANY)
HBM = pl.BlockSpec(memory_space=pltpu.HBM)
PLANES = [(1, 0), (2, 0), (3, 0), (0, 0)]
PLANES += [(f, l) for l in (1, 2) for f in range(4)]
PLANES += [(0, 3), (1, 3), (2, 3), (3, 3)]
OWN = len(PLANES) * ROW
FAR = OWN - 3 * ROW


def reach(f, off):
    return max(0, (4 if f == 0 else 3) - off)


STRIP = [(p, i) for i in range(4) for p, (f, l) in enumerate(PLANES) if i < reach(f, 1 + min(l, 3 - l))]
NEAR = -(-len(STRIP) // 8) * 8
STRIP += [(p, i) for i in range(4) for p, (f, l) in enumerate(PLANES) if i < reach(f, 0) and (p, i) not in STRIP]
TALLY = -(-len(STRIP) // 8) * 8
EDGE = TALLY + 32


def column_table(wide, narrow, wide_axis):
    shape = (wide, narrow) if wide_axis == 0 else (narrow, wide)
    fine = lax.broadcasted_iota(jnp.int32, shape, wide_axis) >> 2
    coarse = lax.broadcasted_iota(jnp.int32, shape, 1 - wide_axis)
    return (fine == coarse).astype(F32).astype(BF16)


def prepare_kernel(
    lowest_ref,
    outer_hbm,
    courant_hbm,
    column_hbm,
    level_hbm,
    value_hbm,
    block_ref,
    field_ref,
    up_ref,
    down_ref,
    outer_ref,
    courant_ref,
    column_ref,
    level_ref,
    value_ref,
    sums_ref,
    sems,
):
    copies = [
        pltpu.make_async_copy(source, target, sems.at[i])
        for i, (source, target) in enumerate(
            (
                (outer_hbm, outer_ref),
                (courant_hbm, courant_ref),
                (column_hbm, column_ref),
                (level_hbm, level_ref),
                (value_hbm, value_ref),
            )
        )
    ]
    for copy in copies:
        copy.start()
    table = column_table(COL * 4, COL, 0)
    copies[1].wait()
    for p, (f, l) in enumerate(PLANES):
        if f > 0:
            block_ref[ROW * p : ROW * p + ROW, :] = courant_ref[f - 1, l].astype(F32)
    for i in (2, 3, 4):
        copies[i].wait()
    observe(lowest_ref[0], column_ref, level_ref, value_ref, field_ref)
    copies[0].wait()
    sums_ref[...] = jnp.dot(
        outer_ref[...].reshape(LEV * ROW * 4, COL * 4), table, preferred_element_type=F32
    )
    for p, (f, l) in enumerate(PLANES):
        if f == 0:
            total = sums_ref[pl.ds(ROW * 4 * l, ROW, stride=4), :]
            for part in range(1, 4):
                total = total + sums_ref[pl.ds(ROW * 4 * l + part, ROW, stride=4), :]
            block_ref[ROW * p : ROW * p + ROW, :] = total * 0.0625
    for ref, edge, step in ((up_ref, ROW - 1, -1), (down_ref, 0, 1)):
        for at, (p, i) in enumerate(STRIP):
            row = ROW * p + edge + step * i
            ref[at : at + 1, :] = block_ref[row : row + 1, :]
        ref[len(STRIP) : TALLY, :] = jnp.zeros((TALLY - len(STRIP), COL), F32)
        for i in range(2):
            begin = TALLY + 16 * i
            ref[begin : begin + 16, :] = field_ref[pl.ds(edge + step * i, 16, stride=ROW), :]


def observe(lowest, column_ref, level_ref, value_ref, field_ref):
    count = column_ref.shape[1]
    chunk = 512
    total = jnp.zeros((4 * COL, COL), F32)
    for begin in range(0, count, chunk):
        cut = slice(begin, begin + chunk)
        cell = column_ref[:, cut]
        place = (level_ref[:, cut] - lowest + 2) * ROW + (cell >> 7)
        value = value_ref[:, cut]
        high = value.astype(BF16).astype(F32)
        rest = value - high
        middle = rest.astype(BF16).astype(F32)
        low = rest - middle
        index = lax.broadcasted_iota(jnp.int32, (COL, chunk), 0)
        here = index == place
        across = jnp.where(index == (cell & 127), 1.0, 0.0).astype(BF16)
        down = jnp.concatenate(
            [jnp.where(here, part, 0.0).astype(BF16) for part in (1.0, high, middle, low)], axis=0
        )
        total = total + lax.dot_general(
            down, across, (((1,), (1,)), ((), ())), preferred_element_type=F32
        )
    field_ref[0:128, :] = total[0:128]
    field_ref[128:256, :] = (total[128:256] + total[256:384]) + total[384:512]


def tile_table():
    own = [(f, l, part) for f in range(4) for l in range(LEV) for part in range(3)]
    first = [(f, l, part) for f, l, part in own if part < 2 or reach(f, 1 + min(l, 3 - l)) > 1]
    tiles = first + [tile for tile in own if tile not in first]
    for f in (4, 5):
        for l in range(1, 7):
            tiles += [(f, l, part) for part in range(3 if 2 <= l < 6 else 2)]
    return tiles, len(first)


TILES, SENT_ON = tile_table()
PACKS = -(-len(TILES) // 32) * 8
ON = -(-SENT_ON // 32) * 8
MORE = 2 * NEAR + 2 * ON


def edges_kernel(block_ref, field_ref, before_ref, after_ref, own_ref, obs_ref, near_ref, right_ref, left_ref):
    for p, (f, l) in enumerate(PLANES):
        own_ref[f, l, 0:ROW, :] = block_ref[ROW * p : ROW * p + ROW, :]
    for f in range(2):
        for l in range(8):
            begin = (f * 8 + l) * ROW
            obs_ref[f, l, 0:ROW, :] = field_ref[begin : begin + ROW, :]
    for side, ref in enumerate((before_ref, after_ref)):
        near_ref[NEAR * side : NEAR * side + NEAR, :] = ref[0:NEAR, :]
        for at, (p, i) in enumerate(STRIP):
            f, l = PLANES[p]
            row = TALL - 1 - i if side == 0 else ROW + i
            own_ref[f, l, row : row + 1, :] = ref[at : at + 1, :]
        for i in range(2):
            row = TALL - 1 - i if side == 0 else ROW + i
            for plane in range(16):
                at = TALLY + 16 * i + plane
                obs_ref[plane // 8, plane % 8, row : row + 1, :] = ref[at : at + 1, :]
    group = lax.broadcasted_iota(jnp.int32, (8, COL), 1) >> 2
    for pack in range(0, PACKS, 8):
        right = jnp.zeros((8, COL), F32)
        left = jnp.zeros((8, COL), F32)
        for slot, (f, l, part) in enumerate(TILES[4 * pack : 4 * pack + 32]):
            ref, f = (own_ref, f) if f < 4 else (obs_ref, f - 4)
            tile = ref[f, l, 8 * part : 8 * part + 8, :]
            right = jnp.where(group == slot, turn(tile, 4 * slot + 4, 1), right)
            left = jnp.where(group == slot, turn(tile, 4 * slot, 1), left)
        right_ref[pack : pack + 8, :] = right
        left_ref[pack : pack + 8, :] = left


def turn(tile, shift, axis):
    shift = shift % tile.shape[axis]
    return pltpu.roll(tile, shift, axis) if shift else tile


def join_kernel(near_ref, west_ref, east_ref, more_ref):
    more_ref[0 : 2 * NEAR, :] = near_ref[...]
    more_ref[2 * NEAR : 2 * NEAR + ON, :] = west_ref[0:ON, :]
    more_ref[2 * NEAR + ON : MORE, :] = east_ref[0:ON, :]


def forward_kernel(parity_ref, pair_ref, later_ref, far_ref):
    del later_ref
    begin = pl.multiple_of((1 - parity_ref[0]) * (3 * ROW), ROW)
    far_ref[...] = pair_ref[pl.ds(begin, FAR), :]


def place_strips(wide_ref, base, ref, start):
    for side in range(2):
        for at, (p, i) in enumerate(STRIP[:NEAR]):
            f, l = PLANES[p]
            if i < reach(f, 1 + min(l, 3 - l)):
                row = TALL - 1 - i if side == 0 else ROW + i
                at += start + NEAR * side
                wide_ref[f, base + l, row : row + 1, 0:COL] = ref[at : at + 1, :]


def place_edges(wide_ref, base, tiles, west, east):
    half = lax.broadcasted_iota(jnp.int32, (8, COL), 1) < 64
    for slot, (f, l, part) in enumerate(tiles):
        pack, lane = divmod(slot, 32)
        level = base + l if f < 4 else 2 + l
        wide_ref[f, level, 8 * part : 8 * part + 8, COL : 2 * COL] = jnp.where(
            half, turn(east(8 * pack), -4 * lane, 1), turn(west(8 * pack), -4 * lane - 4, 1)
        )


def place_more(wide_ref, base, ref, start):
    place_strips(wide_ref, base, ref, start)
    west = start + 2 * NEAR
    place_edges(
        wide_ref,
        base,
        TILES[:SENT_ON],
        lambda row: ref[west + row : west + row + 8, :],
        lambda row: ref[west + ON + row : west + ON + row + 8, :],
    )


def assemble_kernel(
    parity_ref,
    own_ref,
    obs_ref,
    west_ref,
    east_ref,
    pair_ref,
    more_ref,
    wide_ref,
    near_first_ref,
    near_force_ref,
    near_back_ref,
    near_state_ref,
    first_ref,
    force_ref,
):
    wide_ref[0:4, 4:8, :, 0:COL] = own_ref[...]
    wide_ref[4:6, 2:10, :, 0:COL] = obs_ref[...]
    place_edges(
        wide_ref,
        4,
        TILES,
        lambda row: west_ref[row : row + 8, :],
        lambda row: east_ref[row : row + 8, :],
    )
    base = (1 - parity_ref[0]) * 8
    for p, (f, l) in enumerate(PLANES):
        wide_ref[f, base + l, 0:ROW, 0:COL] = pair_ref[ROW * p : ROW * p + ROW, :]
    place_more(wide_ref, base, more_ref, 0)
    parity = parity_ref[0]
    odd = parity == 1

    def field(f, j):
        return wide_ref[f, level_of(parity, j)]

    for j in range(5, 11):
        first_ref[j] = advance(odd, field, lambda i: field(0, i), j)
    for j in range(6, 10):
        state = advance(odd, field, lambda i: first_ref[i], j)
        if j < 8:
            near_state_ref[j - 6] = state[0:ROW, 0:COL]
        force_ref[j] = field(4, j) * state - field(5, j)
    for j in range(7, 9):
        near_back_ref[j - 7] = retreat(odd, field, lambda i: force_ref[i], j)
    near_first_ref[...] = first_ref[5:7]
    near_force_ref[...] = force_ref[6:8]


def plus(x):
    return jnp.maximum(x, 0.0)


def centre(field, j):
    return 1.0 - (jnp.abs(field(1, j)) + jnp.abs(field(2, j)) + jnp.abs(field(3, j)))


def advance(odd, field, get, j):
    here = get(j)
    below, above = jnp.where(odd, get(j + 1), get(j - 1)), jnp.where(odd, get(j - 1), get(j + 1))
    c0, c1, c2 = (field(1 + k, j) for k in range(3))
    result = centre(field, j) * here
    result = result + plus(c0) * below + plus(-c0) * above
    result = result + plus(c1) * turn(here, 1, 0) + plus(-c1) * turn(here, -1, 0)
    return result + plus(c2) * turn(here, 1, 1) + plus(-c2) * turn(here, -1, 1)


def retreat(odd, field, get, j):
    here = get(j)
    sign = jnp.where(odd, -1.0, 1.0)
    c1, c2 = field(2, j), field(3, j)
    result = centre(field, j) * here
    result = result + plus(sign * field(1, j + 1)) * get(j + 1) + plus(-sign * field(1, j - 1)) * get(j - 1)
    result = result + turn(plus(c1) * here, -1, 0) + turn(plus(-c1) * here, 1, 0)
    return result + turn(plus(c2) * here, -1, 1) + turn(plus(-c2) * here, 1, 1)


def level_of(odd, j):
    return j + odd * (11 - 2 * j)


def step_kernel(
    parity_ref,
    given_ref,
    given_first_ref,
    given_force_ref,
    given_back_ref,
    given_state_ref,
    far_ref,
    far_more_ref,
    outer_ref,
    state_ref,
    adjoint_ref,
    next_ref,
    wide_ref,
    first_ref,
    force_ref,
    back_ref,
    flat_ref,
    spread_ref,
):
    parity = parity_ref[0]
    odd = parity == 1
    for p, (f, l) in enumerate(PLANES):
        begin = pl.multiple_of(jnp.clip(ROW * p - (1 - parity) * (3 * ROW), 0, FAR - ROW), ROW)
        wide_ref[f, l, 0:ROW, 0:COL] = far_ref[pl.ds(begin, ROW), :]
    place_more(wide_ref, 0, far_more_ref, 0)

    def field(f, j):
        return wide_ref[f, j + parity * (3 - 2 * j)] if j < 4 else given_ref[f, level_of(parity, j)]

    first_ref[5:7] = given_first_ref[...]
    force_ref[6:8] = given_force_ref[...]
    back_ref[7:9] = given_back_ref[...]
    for j in (6, 7):
        state_ref[level_of(parity, j) - 4] = given_state_ref[j - 6]
    for j in range(1, 5):
        first_ref[j] = advance(odd, field, lambda i: field(0, i), j)
    for j in range(2, 6):
        state = advance(odd, field, lambda i: first_ref[i], j)
        if j >= 4:
            state_ref[level_of(parity, j) - 4] = state[0:ROW, 0:COL]
        level = level_of(parity, j)
        force_ref[j] = given_ref[4, level] * state - given_ref[5, level]
    for j in range(3, 7):
        back_ref[j] = retreat(odd, field, lambda i: force_ref[i], j)
    for j in range(4, 8):
        result = retreat(odd, field, lambda i: back_ref[i], j)[0:ROW, 0:COL]
        place = level_of(parity, j) - 4
        adjoint_ref[place] = result
        flat_ref[pl.ds(pl.multiple_of(place * ROW, ROW), ROW), :] = result
    flat = flat_ref[...]
    high = flat.astype(BF16)
    rest = flat - high.astype(F32)
    middle = rest.astype(BF16)
    low = (rest - middle.astype(F32)).astype(BF16)
    table = column_table(COL * 4, COL, 1)
    spread = jnp.dot(high, table, preferred_element_type=F32)
    spread = spread + jnp.dot(middle, table, preferred_element_type=F32)
    spread = spread + jnp.dot(low, table, preferred_element_type=F32)
    for tile in range(4):
        cut = slice(COL * tile, COL * tile + COL)
        for part in range(4):
            spread_ref[pl.ds(part, LEV * ROW, stride=4), :] = spread[:, cut]
        outer = outer_ref[:, :, cut].astype(F32).reshape(LEV * ROW * 4, COL)
        result = (outer - spread_ref[...]).reshape(LEV, ROW * 4, COL)
        next_ref[:, :, cut] = result.astype(BF16)


def call(kernel, outs, ins, scratch=(), scalars=0, places={}, cost=500000, name=None):
    single = len(outs) == 1
    shapes = [jax.ShapeDtypeStruct(shape, kind) for shape, kind in outs]
    return pl.pallas_call(
        kernel,
        out_shape=shapes[0] if single else shapes,
        in_specs=[SMEM if i < scalars else places.get(i, VMEM) for i in range(len(ins))],
        out_specs=VMEM if single else [VMEM] * len(outs),
        scratch_shapes=list(scratch),
        compiler_params=pltpu.CompilerParams(vmem_limit_bytes=16 * 1024 * 1024),
        cost_estimate=pl.CostEstimate(flops=cost, bytes_accessed=cost, transcendentals=0),
        name=name,
    )(*ins)


def shift(size, by, wrap):
    return [
        (i, (i + by) % size) for i in range(size) if wrap or 0 <= i + by < size
    ]


def shards(outer_increment, courant, obs_column, obs_level, obs_value):
    lev = lax.axis_size("lev")
    lat_up, lat_down = (shift(lax.axis_size("lat"), by, False) for by in (1, -1))
    lon_up, lon_down = (shift(lax.axis_size("lon"), by, True) for by in (1, -1))
    pairs = [(i, i ^ 1) for i in range(lev)]
    far = [(i, i + 2) for i in range(0, lev - 2, 2)] + [(i, i - 2) for i in range(3, lev, 2)]
    position = lax.axis_index("lev").astype(jnp.int32)
    parity = (position & 1).reshape(1)
    lowest = (position * LEV).reshape(1)

    count = obs_column.shape[0]
    given = [outer_increment, courant]
    given += [array.reshape(1, count) for array in (obs_column, obs_level, obs_value)]
    block, fields, up, down = call(
        prepare_kernel,
        [((OWN, COL), F32), ((OWN, COL), F32), ((EDGE, COL), F32), ((EDGE, COL), F32)],
        [lowest] + [pltpu.with_memory_space_constraint(array, pltpu.HBM) for array in given],
        [pltpu.VMEM(array.shape, array.dtype) for array in given]
        + [pltpu.VMEM((LEV * ROW * 4, COL), F32), pltpu.SemaphoreType.DMA((5,))],
        scalars=1,
        places={i: HBM for i in range(1, 6)},
        name="prepare",
    )
    before = lax.ppermute(up, "lat", lat_up)
    after = lax.ppermute(down, "lat", lat_down)
    pair = lax.ppermute(block, "lev", pairs)
    own, obs, near, right, left = call(
        edges_kernel,
        [
            ((4, LEV, TALL, COL), F32),
            ((2, 8, TALL, COL), F32),
            ((2 * NEAR, COL), F32),
            ((PACKS, COL), F32),
            ((PACKS, COL), F32),
        ],
        [block, fields, before, after],
        cost=1000, name="edges",
    )
    west = lax.ppermute(right, "lon", lon_up)
    east = lax.ppermute(left, "lon", lon_down)
    joined = call(join_kernel, [((MORE, COL), F32)], [near, west, east], cost=2000000000, name="join")
    more = lax.ppermute(joined, "lev", pairs)
    onward = call(
        forward_kernel,
        [((FAR, COL), F32)],
        [parity, pair, joined],
        scalars=1,
        places={2: ANY},
        cost=1000, name="forward",
    )
    far_block = lax.ppermute(onward, "lev", far)
    far_more = lax.ppermute(more, "lev", far)
    tall = (DEEP, TALL, 2 * COL)
    plane = (TALL, 2 * COL)
    near = call(
        assemble_kernel,
        [
            ((6,) + tall, F32),
            ((2,) + plane, F32),
            ((2,) + plane, F32),
            ((2,) + plane, F32),
            ((2, ROW, COL), F32),
        ],
        [parity, own, obs, west, east, pair, more],
        [pltpu.VMEM(tall, F32), pltpu.VMEM(tall, F32)],
        scalars=1,
        cost=1000000000, name="assemble",
    )
    state, adjoint, outer_next = call(
        step_kernel,
        [
            ((LEV, ROW, COL), F32),
            ((LEV, ROW, COL), F32),
            (outer_increment.shape, BF16),
        ],
        [parity, *near, far_block, far_more, outer_increment],
        [
            pltpu.VMEM((4, LEV) + plane, F32),
            pltpu.VMEM(tall, F32),
            pltpu.VMEM(tall, F32),
            pltpu.VMEM(tall, F32),
            pltpu.VMEM((LEV * ROW, COL), F32),
            pltpu.VMEM((LEV * ROW * 4, COL), F32),
        ],
        scalars=1,
        name="steps",
    )
    return state, adjoint, outer_next


def solution(mesh):
    placed = (
        P("lev", "lat", "lon"),
        P(None, "lev", "lat", "lon"),
        P(("lat", "lon")),
        P(("lat", "lon")),
        P(("lat", "lon")),
    )
    return jax.shard_map(
        shards,
        mesh=mesh,
        in_specs=placed,
        out_specs=(P("lev", "lat", "lon"), P("lev", "lat", "lon"), P("lev", "lat", "lon")),
        check_vma=False,
    )
```

```python
import jax
import jax.numpy as jnp
from jax import lax
from jax.experimental import pallas as pl
from jax.experimental.pallas import tpu as pltpu
from jax.sharding import PartitionSpec as P

F32 = jnp.float32
BF16 = jnp.bfloat16
VMEM = pl.BlockSpec(memory_space=pltpu.VMEM)
SMEM = pl.BlockSpec(memory_space=pltpu.SMEM)

LEV = 4
ROW = 16
COL = 128
DEEP = 12
TALL = 24
ANY = pl.BlockSpec(memory_space=pl.ANY)
HBM = pl.BlockSpec(memory_space=pltpu.HBM)
PLANES = [(1, 0), (2, 0), (3, 0), (0, 0)]
PLANES += [(f, l) for l in (1, 2) for f in range(4)]
PLANES += [(0, 3), (1, 3), (2, 3), (3, 3)]
OWN = len(PLANES) * ROW
FAR = OWN - 3 * ROW


def reach(f, off):
    return max(0, (4 if f == 0 else 3) - off)


STRIP = [(p, i) for i in range(4) for p, (f, l) in enumerate(PLANES) if i < reach(f, 1 + min(l, 3 - l))]
NEAR = -(-len(STRIP) // 8) * 8
STRIP += [(p, i) for i in range(4) for p, (f, l) in enumerate(PLANES) if i < reach(f, 0) and (p, i) not in STRIP]
TALLY = -(-len(STRIP) // 8) * 8
EDGE = TALLY + 32


def column_table(wide, narrow, wide_axis):
    shape = (wide, narrow) if wide_axis == 0 else (narrow, wide)
    fine = lax.broadcasted_iota(jnp.int32, shape, wide_axis) >> 2
    coarse = lax.broadcasted_iota(jnp.int32, shape, 1 - wide_axis)
    return (fine == coarse).astype(F32).astype(BF16)


def prepare_kernel(
    lowest_ref,
    outer_hbm,
    courant_hbm,
    column_hbm,
    level_hbm,
    value_hbm,
    block_ref,
    field_ref,
    up_ref,
    down_ref,
    outer_ref,
    courant_ref,
    column_ref,
    level_ref,
    value_ref,
    sums_ref,
    sems,
):
    copies = [
        pltpu.make_async_copy(source, target, sems.at[i])
        for i, (source, target) in enumerate(
            (
                (outer_hbm, outer_ref),
                (courant_hbm, courant_ref),
                (column_hbm, column_ref),
                (level_hbm, level_ref),
                (value_hbm, value_ref),
            )
        )
    ]
    for copy in copies:
        copy.start()
    table = column_table(COL * 4, COL, 0)
    copies[1].wait()
    for p, (f, l) in enumerate(PLANES):
        if f > 0:
            block_ref[ROW * p : ROW * p + ROW, :] = courant_ref[f - 1, l].astype(F32)
    for i in (2, 3, 4):
        copies[i].wait()
    observe(lowest_ref[0], column_ref, level_ref, value_ref, field_ref)
    copies[0].wait()
    sums_ref[...] = jnp.dot(
        outer_ref[...].reshape(LEV * ROW * 4, COL * 4), table, preferred_element_type=F32
    )
    for p, (f, l) in enumerate(PLANES):
        if f == 0:
            total = sums_ref[pl.ds(ROW * 4 * l, ROW, stride=4), :]
            for part in range(1, 4):
                total = total + sums_ref[pl.ds(ROW * 4 * l + part, ROW, stride=4), :]
            block_ref[ROW * p : ROW * p + ROW, :] = total * 0.0625
    for ref, edge, step in ((up_ref, ROW - 1, -1), (down_ref, 0, 1)):
        for at, (p, i) in enumerate(STRIP):
            row = ROW * p + edge + step * i
            ref[at : at + 1, :] = block_ref[row : row + 1, :]
        ref[len(STRIP) : TALLY, :] = jnp.zeros((TALLY - len(STRIP), COL), F32)
        for i in range(2):
            begin = TALLY + 16 * i
            ref[begin : begin + 16, :] = field_ref[pl.ds(edge + step * i, 16, stride=ROW), :]


def observe(lowest, column_ref, level_ref, value_ref, field_ref):
    count = column_ref.shape[1]
    chunk = 512
    total = jnp.zeros((4 * COL, COL), F32)
    for begin in range(0, count, chunk):
        cut = slice(begin, begin + chunk)
        cell = column_ref[:, cut]
        place = (level_ref[:, cut] - lowest + 2) * ROW + (cell >> 7)
        value = value_ref[:, cut]
        high = value.astype(BF16)
        rest = value - high.astype(F32)
        middle = rest.astype(BF16)
        low = (rest - middle.astype(F32)).astype(BF16)
        index = lax.broadcasted_iota(jnp.int32, (COL, chunk), 0)
        mask = jnp.where(index == place, 1.0, 0.0).astype(BF16)
        across = jnp.where(index == (cell & 127), 1.0, 0.0).astype(BF16)
        down = jnp.concatenate([mask, mask * high, mask * middle, mask * low], axis=0)
        total = total + lax.dot_general(
            down, across, (((1,), (1,)), ((), ())), preferred_element_type=F32
        )
    field_ref[0:128, :] = total[0:128]
    field_ref[128:256, :] = (total[128:256] + total[256:384]) + total[384:512]


def tile_table():
    own = [(f, l, part) for f in range(4) for l in range(LEV) for part in range(3)]
    first = [(f, l, part) for f, l, part in own if part < 2 or reach(f, 1 + min(l, 3 - l)) > 1]
    tiles = first + [tile for tile in own if tile not in first]
    for f in (4, 5):
        for l in range(1, 7):
            tiles += [(f, l, part) for part in range(3 if 2 <= l < 6 else 2)]
    return tiles, len(first)


TILES, SENT_ON = tile_table()
PACKS = -(-len(TILES) // 32) * 8
ON = -(-SENT_ON // 32) * 8
MORE = 2 * NEAR + 2 * ON


def edges_kernel(block_ref, field_ref, before_ref, after_ref, own_ref, obs_ref, near_ref, right_ref, left_ref):
    for p, (f, l) in enumerate(PLANES):
        own_ref[f, l, 0:ROW, :] = block_ref[ROW * p : ROW * p + ROW, :]
    for f in range(2):
        for l in range(8):
            begin = (f * 8 + l) * ROW
            obs_ref[f, l, 0:ROW, :] = field_ref[begin : begin + ROW, :]
    for side, ref in enumerate((before_ref, after_ref)):
        near_ref[NEAR * side : NEAR * side + NEAR, :] = ref[0:NEAR, :]
        for at, (p, i) in enumerate(STRIP):
            f, l = PLANES[p]
            row = TALL - 1 - i if side == 0 else ROW + i
            own_ref[f, l, row : row + 1, :] = ref[at : at + 1, :]
        for i in range(2):
            row = TALL - 1 - i if side == 0 else ROW + i
            for plane in range(16):
                at = TALLY + 16 * i + plane
                obs_ref[plane // 8, plane % 8, row : row + 1, :] = ref[at : at + 1, :]
    group = lax.broadcasted_iota(jnp.int32, (8, COL), 1) >> 2
    for pack in range(0, PACKS, 8):
        right = jnp.zeros((8, COL), F32)
        left = jnp.zeros((8, COL), F32)
        for slot, (f, l, part) in enumerate(TILES[4 * pack : 4 * pack + 32]):
            ref, f = (own_ref, f) if f < 4 else (obs_ref, f - 4)
            tile = ref[f, l, 8 * part : 8 * part + 8, :]
            right = jnp.where(group == slot, turn(tile, 4 * slot + 4, 1), right)
            left = jnp.where(group == slot, turn(tile, 4 * slot, 1), left)
        right_ref[pack : pack + 8, :] = right
        left_ref[pack : pack + 8, :] = left


def turn(tile, shift, axis):
    shift = shift % tile.shape[axis]
    return pltpu.roll(tile, shift, axis) if shift else tile


def join_kernel(near_ref, west_ref, east_ref, more_ref):
    more_ref[0 : 2 * NEAR, :] = near_ref[...]
    more_ref[2 * NEAR : 2 * NEAR + ON, :] = west_ref[0:ON, :]
    more_ref[2 * NEAR + ON : MORE, :] = east_ref[0:ON, :]


def forward_kernel(parity_ref, pair_ref, later_ref, far_ref):
    del later_ref
    begin = pl.multiple_of((1 - parity_ref[0]) * (3 * ROW), ROW)
    far_ref[...] = pair_ref[pl.ds(begin, FAR), :]


def place_strips(wide_ref, base, ref, start):
    for side in range(2):
        for at, (p, i) in enumerate(STRIP[:NEAR]):
            f, l = PLANES[p]
            if i < reach(f, 1 + min(l, 3 - l)):
                row = TALL - 1 - i if side == 0 else ROW + i
                at += start + NEAR * side
                wide_ref[f, base + l, row : row + 1, 0:COL] = ref[at : at + 1, :]


def place_edges(wide_ref, base, tiles, west, east):
    half = lax.broadcasted_iota(jnp.int32, (8, COL), 1) < 64
    for slot, (f, l, part) in enumerate(tiles):
        pack, lane = divmod(slot, 32)
        level = base + l if f < 4 else 2 + l
        wide_ref[f, level, 8 * part : 8 * part + 8, COL : 2 * COL] = jnp.where(
            half, turn(east(8 * pack), -4 * lane, 1), turn(west(8 * pack), -4 * lane - 4, 1)
        )


def place_more(wide_ref, base, ref, start):
    place_strips(wide_ref, base, ref, start)
    west = start + 2 * NEAR
    place_edges(
        wide_ref,
        base,
        TILES[:SENT_ON],
        lambda row: ref[west + row : west + row + 8, :],
        lambda row: ref[west + ON + row : west + ON + row + 8, :],
    )


def assemble_kernel(
    parity_ref,
    own_ref,
    obs_ref,
    west_ref,
    east_ref,
    pair_ref,
    more_ref,
    wide_ref,
    near_first_ref,
    near_force_ref,
    near_back_ref,
    near_state_ref,
    first_ref,
    force_ref,
):
    wide_ref[0:4, 4:8, :, 0:COL] = own_ref[...]
    wide_ref[4:6, 2:10, :, 0:COL] = obs_ref[...]
    place_edges(
        wide_ref,
        4,
        TILES,
        lambda row: west_ref[row : row + 8, :],
        lambda row: east_ref[row : row + 8, :],
    )
    base = (1 - parity_ref[0]) * 8
    for p, (f, l) in enumerate(PLANES):
        wide_ref[f, base + l, 0:ROW, 0:COL] = pair_ref[ROW * p : ROW * p + ROW, :]
    place_more(wide_ref, base, more_ref, 0)
    parity = parity_ref[0]
    odd = parity == 1

    def field(f, j):
        return wide_ref[f, level_of(parity, j)]

    for j in range(5, 11):
        first_ref[j] = advance(odd, field, lambda i: field(0, i), j)
    for j in range(6, 10):
        state = advance(odd, field, lambda i: first_ref[i], j)
        if j < 8:
            near_state_ref[j - 6] = state[0:ROW, 0:COL]
        force_ref[j] = field(4, j) * state - field(5, j)
    for j in range(7, 9):
        near_back_ref[j - 7] = retreat(odd, field, lambda i: force_ref[i], j)
    near_first_ref[...] = first_ref[5:7]
    near_force_ref[...] = force_ref[6:8]


def plus(x):
    return jnp.maximum(x, 0.0)


def centre(field, j):
    return 1.0 - (jnp.abs(field(1, j)) + jnp.abs(field(2, j)) + jnp.abs(field(3, j)))


def advance(odd, field, get, j):
    here = get(j)
    below, above = jnp.where(odd, get(j + 1), get(j - 1)), jnp.where(odd, get(j - 1), get(j + 1))
    c0, c1, c2 = (field(1 + k, j) for k in range(3))
    result = centre(field, j) * here
    result = result + plus(c0) * below + plus(-c0) * above
    result = result + plus(c1) * turn(here, 1, 0) + plus(-c1) * turn(here, -1, 0)
    return result + plus(c2) * turn(here, 1, 1) + plus(-c2) * turn(here, -1, 1)


def retreat(odd, field, get, j):
    here = get(j)
    sign = jnp.where(odd, -1.0, 1.0)
    c1, c2 = field(2, j), field(3, j)
    result = centre(field, j) * here
    result = result + plus(sign * field(1, j + 1)) * get(j + 1) + plus(-sign * field(1, j - 1)) * get(j - 1)
    result = result + turn(plus(c1) * here, -1, 0) + turn(plus(-c1) * here, 1, 0)
    return result + turn(plus(c2) * here, -1, 1) + turn(plus(-c2) * here, 1, 1)


def level_of(odd, j):
    return j + odd * (11 - 2 * j)


def step_kernel(
    parity_ref,
    given_ref,
    given_first_ref,
    given_force_ref,
    given_back_ref,
    given_state_ref,
    far_ref,
    far_more_ref,
    outer_ref,
    state_ref,
    adjoint_ref,
    next_ref,
    wide_ref,
    first_ref,
    force_ref,
    back_ref,
    flat_ref,
    spread_ref,
):
    parity = parity_ref[0]
    odd = parity == 1
    for p, (f, l) in enumerate(PLANES):
        begin = pl.multiple_of(jnp.clip(ROW * p - (1 - parity) * (3 * ROW), 0, FAR - ROW), ROW)
        wide_ref[f, l, 0:ROW, 0:COL] = far_ref[pl.ds(begin, ROW), :]
    place_more(wide_ref, 0, far_more_ref, 0)

    def field(f, j):
        return wide_ref[f, j + parity * (3 - 2 * j)] if j < 4 else given_ref[f, level_of(parity, j)]

    first_ref[5:7] = given_first_ref[...]
    force_ref[6:8] = given_force_ref[...]
    back_ref[7:9] = given_back_ref[...]
    for j in (6, 7):
        state_ref[level_of(parity, j) - 4] = given_state_ref[j - 6]
    for j in range(1, 5):
        first_ref[j] = advance(odd, field, lambda i: field(0, i), j)
    for j in range(2, 6):
        state = advance(odd, field, lambda i: first_ref[i], j)
        if j >= 4:
            state_ref[level_of(parity, j) - 4] = state[0:ROW, 0:COL]
        level = level_of(parity, j)
        force_ref[j] = given_ref[4, level] * state - given_ref[5, level]
    for j in range(3, 7):
        back_ref[j] = retreat(odd, field, lambda i: force_ref[i], j)
    for j in range(4, 8):
        result = retreat(odd, field, lambda i: back_ref[i], j)[0:ROW, 0:COL]
        place = level_of(parity, j) - 4
        adjoint_ref[place] = result
        flat_ref[pl.ds(pl.multiple_of(place * ROW, ROW), ROW), :] = result
    flat = flat_ref[...]
    high = flat.astype(BF16)
    rest = flat - high.astype(F32)
    middle = rest.astype(BF16)
    low = (rest - middle.astype(F32)).astype(BF16)
    table = column_table(COL * 4, COL, 1)
    spread = jnp.dot(high, table, preferred_element_type=F32)
    spread = spread + jnp.dot(middle, table, preferred_element_type=F32)
    spread = spread + jnp.dot(low, table, preferred_element_type=F32)
    for tile in range(4):
        cut = slice(COL * tile, COL * tile + COL)
        for part in range(4):
            spread_ref[pl.ds(part, LEV * ROW, stride=4), :] = spread[:, cut]
        outer = outer_ref[:, :, cut].astype(F32).reshape(LEV * ROW * 4, COL)
        result = (outer - spread_ref[...]).reshape(LEV, ROW * 4, COL)
        next_ref[:, :, cut] = result.astype(BF16)


def call(kernel, outs, ins, scratch=(), scalars=0, places={}, cost=500000, name=None):
    single = len(outs) == 1
    shapes = [jax.ShapeDtypeStruct(shape, kind) for shape, kind in outs]
    return pl.pallas_call(
        kernel,
        out_shape=shapes[0] if single else shapes,
        in_specs=[SMEM if i < scalars else places.get(i, VMEM) for i in range(len(ins))],
        out_specs=VMEM if single else [VMEM] * len(outs),
        scratch_shapes=list(scratch),
        compiler_params=pltpu.CompilerParams(vmem_limit_bytes=16 * 1024 * 1024),
        cost_estimate=pl.CostEstimate(flops=cost, bytes_accessed=cost, transcendentals=0),
        name=name,
    )(*ins)


def shift(size, by, wrap):
    return [
        (i, (i + by) % size) for i in range(size) if wrap or 0 <= i + by < size
    ]


def shards(outer_increment, courant, obs_column, obs_level, obs_value):
    lev = lax.axis_size("lev")
    lat_up, lat_down = (shift(lax.axis_size("lat"), by, False) for by in (1, -1))
    lon_up, lon_down = (shift(lax.axis_size("lon"), by, True) for by in (1, -1))
    pairs = [(i, i ^ 1) for i in range(lev)]
    far = [(i, i + 2) for i in range(0, lev - 2, 2)] + [(i, i - 2) for i in range(3, lev, 2)]
    position = lax.axis_index("lev").astype(jnp.int32)
    parity = (position & 1).reshape(1)
    lowest = (position * LEV).reshape(1)

    count = obs_column.shape[0]
    given = [outer_increment, courant]
    given += [array.reshape(1, count) for array in (obs_column, obs_level, obs_value)]
    block, fields, up, down = call(
        prepare_kernel,
        [((OWN, COL), F32), ((OWN, COL), F32), ((EDGE, COL), F32), ((EDGE, COL), F32)],
        [lowest] + [pltpu.with_memory_space_constraint(array, pltpu.HBM) for array in given],
        [pltpu.VMEM(array.shape, array.dtype) for array in given]
        + [pltpu.VMEM((LEV * ROW * 4, COL), F32), pltpu.SemaphoreType.DMA((5,))],
        scalars=1,
        places={i: HBM for i in range(1, 6)},
        name="prepare",
    )
    before = lax.ppermute(up, "lat", lat_up)
    after = lax.ppermute(down, "lat", lat_down)
    pair = lax.ppermute(block, "lev", pairs)
    own, obs, near, right, left = call(
        edges_kernel,
        [
            ((4, LEV, TALL, COL), F32),
            ((2, 8, TALL, COL), F32),
            ((2 * NEAR, COL), F32),
            ((PACKS, COL), F32),
            ((PACKS, COL), F32),
        ],
        [block, fields, before, after],
        cost=2000000000, name="edges",
    )
    west = lax.ppermute(right, "lon", lon_up)
    east = lax.ppermute(left, "lon", lon_down)
    joined = call(join_kernel, [((MORE, COL), F32)], [near, west, east], cost=1000, name="join")
    more = lax.ppermute(joined, "lev", pairs)
    onward = call(
        forward_kernel,
        [((FAR, COL), F32)],
        [parity, pair, joined],
        scalars=1,
        places={2: ANY},
        cost=1000, name="forward",
    )
    far_block = lax.ppermute(onward, "lev", far)
    far_more = lax.ppermute(more, "lev", far)
    tall = (DEEP, TALL, 2 * COL)
    plane = (TALL, 2 * COL)
    near = call(
        assemble_kernel,
        [
            ((6,) + tall, F32),
            ((2,) + plane, F32),
            ((2,) + plane, F32),
            ((2,) + plane, F32),
            ((2, ROW, COL), F32),
        ],
        [parity, own, obs, west, east, pair, more],
        [pltpu.VMEM(tall, F32), pltpu.VMEM(tall, F32)],
        scalars=1,
        cost=1000000000,
        name="assemble",
    )
    state, adjoint, outer_next = call(
        step_kernel,
        [
            ((LEV, ROW, COL), F32),
            ((LEV, ROW, COL), F32),
            (outer_increment.shape, BF16),
        ],
        [parity, *near, far_block, far_more, outer_increment],
        [
            pltpu.VMEM((4, LEV) + plane, F32),
            pltpu.VMEM(tall, F32),
            pltpu.VMEM(tall, F32),
            pltpu.VMEM(tall, F32),
            pltpu.VMEM((LEV * ROW, COL), F32),
            pltpu.VMEM((LEV * ROW * 4, COL), F32),
        ],
        scalars=1,
        name="steps",
    )
    return state, adjoint, outer_next


def solution(mesh):
    placed = (
        P("lev", "lat", "lon"),
        P(None, "lev", "lat", "lon"),
        P(("lat", "lon")),
        P(("lat", "lon")),
        P(("lat", "lon")),
    )
    return jax.shard_map(
        shards,
        mesh=mesh,
        in_specs=placed,
        out_specs=(P("lev", "lat", "lon"), P("lev", "lat", "lon"), P("lev", "lat", "lon")),
        check_vma=False,
    )
```

```python
import jax
import jax.numpy as jnp
from jax import lax
from jax.experimental import pallas as pl
from jax.experimental.pallas import tpu as pltpu
from jax.sharding import PartitionSpec as P

F32 = jnp.float32
BF16 = jnp.bfloat16
VMEM = pl.BlockSpec(memory_space=pltpu.VMEM)
SMEM = pl.BlockSpec(memory_space=pltpu.SMEM)

LEV = 4
ROW = 16
COL = 128
DEEP = 12
TALL = 24
ANY = pl.BlockSpec(memory_space=pl.ANY)
HBM = pl.BlockSpec(memory_space=pltpu.HBM)
PLANES = [(1, 0), (2, 0), (3, 0), (0, 0)]
PLANES += [(f, l) for l in (1, 2) for f in range(4)]
PLANES += [(0, 3), (1, 3), (2, 3), (3, 3)]
OWN = len(PLANES) * ROW
FAR = OWN - 3 * ROW


def reach(f, off):
    return max(0, (4 if f == 0 else 3) - off)


STRIP = [(p, i) for i in range(4) for p, (f, l) in enumerate(PLANES) if i < reach(f, 1 + min(l, 3 - l))]
NEAR = -(-len(STRIP) // 8) * 8
STRIP += [(p, i) for i in range(4) for p, (f, l) in enumerate(PLANES) if i < reach(f, 0) and (p, i) not in STRIP]
TALLY = -(-len(STRIP) // 8) * 8
EDGE = TALLY + 32


def column_table(wide, narrow, wide_axis):
    shape = (wide, narrow) if wide_axis == 0 else (narrow, wide)
    fine = lax.broadcasted_iota(jnp.int32, shape, wide_axis) >> 2
    coarse = lax.broadcasted_iota(jnp.int32, shape, 1 - wide_axis)
    return (fine == coarse).astype(F32).astype(BF16)


def prepare_kernel(
    lowest_ref,
    outer_hbm,
    courant_hbm,
    column_hbm,
    level_hbm,
    value_hbm,
    block_ref,
    field_ref,
    up_ref,
    down_ref,
    outer_ref,
    courant_ref,
    column_ref,
    level_ref,
    value_ref,
    sums_ref,
    sems,
):
    copies = [
        pltpu.make_async_copy(source, target, sems.at[i])
        for i, (source, target) in enumerate(
            (
                (outer_hbm, outer_ref),
                (courant_hbm, courant_ref),
                (column_hbm, column_ref),
                (level_hbm, level_ref),
                (value_hbm, value_ref),
            )
        )
    ]
    for copy in copies:
        copy.start()
    table = column_table(COL * 4, COL, 0)
    copies[1].wait()
    for p, (f, l) in enumerate(PLANES):
        if f > 0:
            block_ref[ROW * p : ROW * p + ROW, :] = courant_ref[f - 1, l].astype(F32)
    for i in (2, 3, 4):
        copies[i].wait()
    observe(lowest_ref[0], column_ref, level_ref, value_ref, field_ref)
    copies[0].wait()
    sums_ref[...] = jnp.dot(
        outer_ref[...].reshape(LEV * ROW * 4, COL * 4), table, preferred_element_type=F32
    )
    for p, (f, l) in enumerate(PLANES):
        if f == 0:
            total = sums_ref[pl.ds(ROW * 4 * l, ROW, stride=4), :]
            for part in range(1, 4):
                total = total + sums_ref[pl.ds(ROW * 4 * l + part, ROW, stride=4), :]
            block_ref[ROW * p : ROW * p + ROW, :] = total * 0.0625
    for ref, edge, step in ((up_ref, ROW - 1, -1), (down_ref, 0, 1)):
        for at, (p, i) in enumerate(STRIP):
            row = ROW * p + edge + step * i
            ref[at : at + 1, :] = block_ref[row : row + 1, :]
        ref[len(STRIP) : TALLY, :] = jnp.zeros((TALLY - len(STRIP), COL), F32)
        for i in range(2):
            begin = TALLY + 16 * i
            ref[begin : begin + 16, :] = field_ref[pl.ds(edge + step * i, 16, stride=ROW), :]


def observe(lowest, column_ref, level_ref, value_ref, field_ref):
    count = column_ref.shape[1]
    chunk = 512
    total = jnp.zeros((4 * COL, COL), F32)
    for begin in range(0, count, chunk):
        cut = slice(begin, begin + chunk)
        cell = column_ref[:, cut]
        place = (level_ref[:, cut] - lowest + 2) * ROW + (cell >> 7)
        value = value_ref[:, cut]
        high = value.astype(BF16)
        rest = value - high.astype(F32)
        middle = rest.astype(BF16)
        low = (rest - middle.astype(F32)).astype(BF16)
        index = lax.broadcasted_iota(jnp.int32, (COL, chunk), 0)
        mask = jnp.where(index == place, 1.0, 0.0).astype(BF16)
        across = jnp.where(index == (cell & 127), 1.0, 0.0).astype(BF16)
        down = jnp.concatenate([mask, mask * high, mask * middle, mask * low], axis=0)
        total = total + lax.dot_general(
            down, across, (((1,), (1,)), ((), ())), preferred_element_type=F32
        )
    field_ref[0:128, :] = total[0:128]
    field_ref[128:256, :] = (total[128:256] + total[256:384]) + total[384:512]


def tile_table():
    own = [(f, l, part) for f in range(4) for l in range(LEV) for part in range(3)]
    first = [(f, l, part) for f, l, part in own if part < 2 or reach(f, 1 + min(l, 3 - l)) > 1]
    tiles = first + [tile for tile in own if tile not in first]
    for f in (4, 5):
        for l in range(1, 7):
            tiles += [(f, l, part) for part in range(3 if 2 <= l < 6 else 2)]
    return tiles, len(first)


TILES, SENT_ON = tile_table()
PACKS = -(-len(TILES) // 32) * 8
ON = -(-SENT_ON // 32) * 8
MORE = 2 * NEAR + 2 * ON


def edges_kernel(block_ref, field_ref, before_ref, after_ref, own_ref, obs_ref, near_ref, right_ref, left_ref):
    for p, (f, l) in enumerate(PLANES):
        own_ref[f, l, 0:ROW, :] = block_ref[ROW * p : ROW * p + ROW, :]
    for f in range(2):
        for l in range(8):
            begin = (f * 8 + l) * ROW
            obs_ref[f, l, 0:ROW, :] = field_ref[begin : begin + ROW, :]
    for side, ref in enumerate((before_ref, after_ref)):
        near_ref[NEAR * side : NEAR * side + NEAR, :] = ref[0:NEAR, :]
        for at, (p, i) in enumerate(STRIP):
            f, l = PLANES[p]
            row = TALL - 1 - i if side == 0 else ROW + i
            own_ref[f, l, row : row + 1, :] = ref[at : at + 1, :]
        for i in range(2):
            row = TALL - 1 - i if side == 0 else ROW + i
            for plane in range(16):
                at = TALLY + 16 * i + plane
                obs_ref[plane // 8, plane % 8, row : row + 1, :] = ref[at : at + 1, :]
    group = lax.broadcasted_iota(jnp.int32, (8, COL), 1) >> 2
    for pack in range(0, PACKS, 8):
        right = jnp.zeros((8, COL), F32)
        left = jnp.zeros((8, COL), F32)
        for slot, (f, l, part) in enumerate(TILES[4 * pack : 4 * pack + 32]):
            ref, f = (own_ref, f) if f < 4 else (obs_ref, f - 4)
            tile = ref[f, l, 8 * part : 8 * part + 8, :]
            right = jnp.where(group == slot, turn(tile, 4 * slot + 4, 1), right)
            left = jnp.where(group == slot, turn(tile, 4 * slot, 1), left)
        right_ref[pack : pack + 8, :] = right
        left_ref[pack : pack + 8, :] = left


def turn(tile, shift, axis):
    shift = shift % tile.shape[axis]
    return pltpu.roll(tile, shift, axis) if shift else tile


def join_kernel(near_ref, west_ref, east_ref, more_ref):
    more_ref[0 : 2 * NEAR, :] = near_ref[...]
    more_ref[2 * NEAR : 2 * NEAR + ON, :] = west_ref[0:ON, :]
    more_ref[2 * NEAR + ON : MORE, :] = east_ref[0:ON, :]


def forward_kernel(parity_ref, pair_ref, later_ref, far_ref):
    del later_ref
    begin = pl.multiple_of((1 - parity_ref[0]) * (3 * ROW), ROW)
    far_ref[...] = pair_ref[pl.ds(begin, FAR), :]


def place_strips(wide_ref, base, ref, start):
    for side in range(2):
        for at, (p, i) in enumerate(STRIP[:NEAR]):
            f, l = PLANES[p]
            if i < reach(f, 1 + min(l, 3 - l)):
                row = TALL - 1 - i if side == 0 else ROW + i
                at += start + NEAR * side
                wide_ref[f, base + l, row : row + 1, 0:COL] = ref[at : at + 1, :]


def place_edges(wide_ref, base, tiles, west, east):
    half = lax.broadcasted_iota(jnp.int32, (8, COL), 1) < 64
    for slot, (f, l, part) in enumerate(tiles):
        pack, lane = divmod(slot, 32)
        level = base + l if f < 4 else 2 + l
        wide_ref[f, level, 8 * part : 8 * part + 8, COL : 2 * COL] = jnp.where(
            half, turn(east(8 * pack), -4 * lane, 1), turn(west(8 * pack), -4 * lane - 4, 1)
        )


def place_more(wide_ref, base, ref, start):
    place_strips(wide_ref, base, ref, start)
    west = start + 2 * NEAR
    place_edges(
        wide_ref,
        base,
        TILES[:SENT_ON],
        lambda row: ref[west + row : west + row + 8, :],
        lambda row: ref[west + ON + row : west + ON + row + 8, :],
    )


def assemble_kernel(
    parity_ref,
    own_ref,
    obs_ref,
    west_ref,
    east_ref,
    pair_ref,
    more_ref,
    wide_ref,
    near_first_ref,
    near_force_ref,
    near_back_ref,
    near_state_ref,
    first_ref,
    force_ref,
):
    wide_ref[0:4, 4:8, :, 0:COL] = own_ref[...]
    wide_ref[4:6, 2:10, :, 0:COL] = obs_ref[...]
    place_edges(
        wide_ref,
        4,
        TILES,
        lambda row: west_ref[row : row + 8, :],
        lambda row: east_ref[row : row + 8, :],
    )
    base = (1 - parity_ref[0]) * 8
    for p, (f, l) in enumerate(PLANES):
        wide_ref[f, base + l, 0:ROW, 0:COL] = pair_ref[ROW * p : ROW * p + ROW, :]
    place_more(wide_ref, base, more_ref, 0)
    parity = parity_ref[0]
    odd = parity == 1

    def field(f, j):
        return wide_ref[f, level_of(parity, j)]

    for j in range(5, 11):
        first_ref[j] = advance(odd, field, lambda i: field(0, i), j)
    for j in range(6, 10):
        state = advance(odd, field, lambda i: first_ref[i], j)
        if j < 8:
            near_state_ref[j - 6] = state[0:ROW, 0:COL]
        force_ref[j] = field(4, j) * state - field(5, j)
    for j in range(7, 9):
        near_back_ref[j - 7] = retreat(odd, field, lambda i: force_ref[i], j)
    near_first_ref[...] = first_ref[5:7]
    near_force_ref[...] = force_ref[6:8]


def plus(x):
    return jnp.maximum(x, 0.0)


def centre(field, j):
    return 1.0 - (jnp.abs(field(1, j)) + jnp.abs(field(2, j)) + jnp.abs(field(3, j)))


def advance(odd, field, get, j):
    here = get(j)
    below, above = jnp.where(odd, get(j + 1), get(j - 1)), jnp.where(odd, get(j - 1), get(j + 1))
    c0, c1, c2 = (field(1 + k, j) for k in range(3))
    result = centre(field, j) * here
    result = result + plus(c0) * below + plus(-c0) * above
    result = result + plus(c1) * turn(here, 1, 0) + plus(-c1) * turn(here, -1, 0)
    return result + plus(c2) * turn(here, 1, 1) + plus(-c2) * turn(here, -1, 1)


def retreat(odd, field, get, j):
    here = get(j)
    sign = jnp.where(odd, -1.0, 1.0)
    c1, c2 = field(2, j), field(3, j)
    result = centre(field, j) * here
    result = result + plus(sign * field(1, j + 1)) * get(j + 1) + plus(-sign * field(1, j - 1)) * get(j - 1)
    result = result + turn(plus(c1) * here, -1, 0) + turn(plus(-c1) * here, 1, 0)
    return result + turn(plus(c2) * here, -1, 1) + turn(plus(-c2) * here, 1, 1)


def level_of(odd, j):
    return j + odd * (11 - 2 * j)


def step_kernel(
    parity_ref,
    given_ref,
    given_first_ref,
    given_force_ref,
    given_back_ref,
    given_state_ref,
    far_ref,
    far_more_ref,
    outer_ref,
    state_ref,
    adjoint_ref,
    next_ref,
    wide_ref,
    first_ref,
    force_ref,
    back_ref,
    flat_ref,
    spread_ref,
):
    parity = parity_ref[0]
    odd = parity == 1
    for p, (f, l) in enumerate(PLANES):
        begin = pl.multiple_of(jnp.clip(ROW * p - (1 - parity) * (3 * ROW), 0, FAR - ROW), ROW)
        wide_ref[f, l, 0:ROW, 0:COL] = far_ref[pl.ds(begin, ROW), :]
    place_more(wide_ref, 0, far_more_ref, 0)

    def field(f, j):
        return wide_ref[f, j + parity * (3 - 2 * j)] if j < 4 else given_ref[f, level_of(parity, j)]

    first_ref[5:7] = given_first_ref[...]
    force_ref[6:8] = given_force_ref[...]
    back_ref[7:9] = given_back_ref[...]
    for j in (6, 7):
        state_ref[level_of(parity, j) - 4] = given_state_ref[j - 6]
    for j in range(1, 5):
        first_ref[j] = advance(odd, field, lambda i: field(0, i), j)
    for j in range(2, 6):
        state = advance(odd, field, lambda i: first_ref[i], j)
        if j >= 4:
            state_ref[level_of(parity, j) - 4] = state[0:ROW, 0:COL]
        level = level_of(parity, j)
        force_ref[j] = given_ref[4, level] * state - given_ref[5, level]
    for j in range(3, 7):
        back_ref[j] = retreat(odd, field, lambda i: force_ref[i], j)
    for j in range(4, 8):
        result = retreat(odd, field, lambda i: back_ref[i], j)[0:ROW, 0:COL]
        place = level_of(parity, j) - 4
        adjoint_ref[place] = result
        flat_ref[pl.ds(pl.multiple_of(place * ROW, ROW), ROW), :] = result
    flat = flat_ref[...]
    high = flat.astype(BF16)
    rest = flat - high.astype(F32)
    middle = rest.astype(BF16)
    low = (rest - middle.astype(F32)).astype(BF16)
    table = column_table(COL * 4, COL, 1)
    spread = jnp.dot(high, table, preferred_element_type=F32)
    spread = spread + jnp.dot(middle, table, preferred_element_type=F32)
    spread = spread + jnp.dot(low, table, preferred_element_type=F32)
    for tile in range(4):
        cut = slice(COL * tile, COL * tile + COL)
        for part in range(4):
            spread_ref[pl.ds(part, LEV * ROW, stride=4), :] = spread[:, cut]
        outer = outer_ref[:, :, cut].astype(F32).reshape(LEV * ROW * 4, COL)
        result = (outer - spread_ref[...]).reshape(LEV, ROW * 4, COL)
        next_ref[:, :, cut] = result.astype(BF16)


def call(kernel, outs, ins, scratch=(), scalars=0, places={}, cost=500000, name=None):
    single = len(outs) == 1
    shapes = [jax.ShapeDtypeStruct(shape, kind) for shape, kind in outs]
    return pl.pallas_call(
        kernel,
        out_shape=shapes[0] if single else shapes,
        in_specs=[SMEM if i < scalars else places.get(i, VMEM) for i in range(len(ins))],
        out_specs=VMEM if single else [VMEM] * len(outs),
        scratch_shapes=list(scratch),
        compiler_params=pltpu.CompilerParams(vmem_limit_bytes=16 * 1024 * 1024),
        cost_estimate=pl.CostEstimate(flops=cost, bytes_accessed=cost, transcendentals=0),
        name=name,
    )(*ins)


def exchange(upper, lower, axis, wrap):
    size = lax.axis_size(axis)
    even = (lax.axis_index(axis) & 1) == 0
    first = [(i, i ^ 1) for i in range(size)]
    second = [(i, i + 1 if i % 2 else i - 1) for i in range(size)]
    second = [(i, j % size) for i, j in second if wrap or 0 <= j < size]
    one = lax.ppermute(jnp.where(even, upper, lower), axis, first)
    two = lax.ppermute(jnp.where(even, lower, upper), axis, second)
    return jnp.where(even, two, one), jnp.where(even, one, two)


def shards(outer_increment, courant, obs_column, obs_level, obs_value):
    lev = lax.axis_size("lev")
    pairs = [(i, i ^ 1) for i in range(lev)]
    far = [(i, i + 2) for i in range(0, lev - 2, 2)] + [(i, i - 2) for i in range(3, lev, 2)]
    position = lax.axis_index("lev").astype(jnp.int32)
    parity = (position & 1).reshape(1)
    lowest = (position * LEV).reshape(1)

    count = obs_column.shape[0]
    given = [outer_increment, courant]
    given += [array.reshape(1, count) for array in (obs_column, obs_level, obs_value)]
    block, fields, up, down = call(
        prepare_kernel,
        [((OWN, COL), F32), ((OWN, COL), F32), ((EDGE, COL), F32), ((EDGE, COL), F32)],
        [lowest] + [pltpu.with_memory_space_constraint(array, pltpu.HBM) for array in given],
        [pltpu.VMEM(array.shape, array.dtype) for array in given]
        + [pltpu.VMEM((LEV * ROW * 4, COL), F32), pltpu.SemaphoreType.DMA((5,))],
        scalars=1,
        places={i: HBM for i in range(1, 6)},
        name="prepare",
    )
    before, after = exchange(up, down, "lat", False)
    pair = lax.ppermute(block, "lev", pairs)
    own, obs, near, right, left = call(
        edges_kernel,
        [
            ((4, LEV, TALL, COL), F32),
            ((2, 8, TALL, COL), F32),
            ((2 * NEAR, COL), F32),
            ((PACKS, COL), F32),
            ((PACKS, COL), F32),
        ],
        [block, fields, before, after],
        cost=2000000000, name="edges",
    )
    lon = lax.axis_size("lon")
    west = lax.ppermute(right, "lon", [(i, (i + 1) % lon) for i in range(lon)])
    east = lax.ppermute(left, "lon", [(i, (i - 1) % lon) for i in range(lon)])
    joined = call(join_kernel, [((MORE, COL), F32)], [near, west, east], cost=1000, name="join")
    more = lax.ppermute(joined, "lev", pairs)
    onward = call(
        forward_kernel,
        [((FAR, COL), F32)],
        [parity, pair, joined],
        scalars=1,
        places={2: ANY},
        cost=1000, name="forward",
    )
    far_block = lax.ppermute(onward, "lev", far)
    far_more = lax.ppermute(more, "lev", far)
    tall = (DEEP, TALL, 2 * COL)
    plane = (TALL, 2 * COL)
    near = call(
        assemble_kernel,
        [
            ((6,) + tall, F32),
            ((2,) + plane, F32),
            ((2,) + plane, F32),
            ((2,) + plane, F32),
            ((2, ROW, COL), F32),
        ],
        [parity, own, obs, west, east, pair, more],
        [pltpu.VMEM(tall, F32), pltpu.VMEM(tall, F32)],
        scalars=1,
        cost=1000000000,
        name="assemble",
    )
    state, adjoint, outer_next = call(
        step_kernel,
        [
            ((LEV, ROW, COL), F32),
            ((LEV, ROW, COL), F32),
            (outer_increment.shape, BF16),
        ],
        [parity, *near, far_block, far_more, outer_increment],
        [
            pltpu.VMEM((4, LEV) + plane, F32),
            pltpu.VMEM(tall, F32),
            pltpu.VMEM(tall, F32),
            pltpu.VMEM(tall, F32),
            pltpu.VMEM((LEV * ROW, COL), F32),
            pltpu.VMEM((LEV * ROW * 4, COL), F32),
        ],
        scalars=1,
        name="steps",
    )
    return state, adjoint, outer_next


def solution(mesh):
    placed = (
        P("lev", "lat", "lon"),
        P(None, "lev", "lat", "lon"),
        P(("lat", "lon")),
        P(("lat", "lon")),
        P(("lat", "lon")),
    )
    return jax.shard_map(
        shards,
        mesh=mesh,
        in_specs=placed,
        out_specs=(P("lev", "lat", "lon"), P("lev", "lat", "lon"), P("lev", "lat", "lon")),
        check_vma=False,
    )
```
